256 devices in a mesh: dp: 2 (over core), frame: 16 (over x, y), mp: 8 (over z).
Axes of the slice: x: 4, y: 4, z: 8, core: 2. Of those that a mesh axis runs over, the one named last changes fastest.
Arguments:
- frames_in: bfloat16 [2, 16, 1024, 768], P('dp', 'frame'), may hold values from -6 to 6
- gain_space: float32 [768], replicated, may hold values from 0.1 to 1.9
- space_proj: bfloat16 [3, 768, 512], P(None, None, 'mp'), may hold values from -0.21875 to 0.21875
- space_out: bfloat16 [512, 768], replicated, may hold values from -0.25 to 0.25
- gain_time: float32 [768], replicated, may hold values from 0.1 to 1.9
- time_proj: bfloat16 [3, 768, 768], replicated, may hold values from -0.21875 to 0.21875
- time_out: bfloat16 [768, 768], replicated, may hold values from -0.21875 to 0.21875
- gain_mlp: float32 [768], replicated, may hold values from 0.1 to 1.9
- mlp_in: bfloat16 [3072, 768], P(('frame', 'mp')), may hold values from -0.21875 to 0.21875
- mlp_out: bfloat16 [3072, 768], P(('frame', 'mp')), may hold values from -0.109375 to 0.109375
- code_proj: bfloat16 [768, 32], replicated, may hold values from -0.21875 to 0.21875
- code_index: int32 [2, 16, 1024], P('dp', None, ('frame', 'mp')), may hold values from 0 to 1023, as said below
Outputs:
- block_out: bfloat16 [2, 16, 1024, 768], P('dp', None, ('frame', 'mp'))
- code_means: float32 [1024, 32], replicated
The draws below stay inside these ranges and needn't reach their ends.
Inputs may be any that keep to these rules, and one draw needn't show every extreme that they name: `code_index`: at least 128 codes are named by no token; which ones is drawn from the seed.
All inputs are finite; a program needn't handle non-finite values.
Results may differ from the reference program's by a relative error of at most 0.017.
Values may be sent and summed in bfloat16 or wider, within the bound.
A program may use at most 64 MiB of HBM per device.

```python
import math
import jax
import jax.numpy as jnp
from jax import lax

D = 768
HD = 64
T_HEADS = 12
S_HEADS = 8
FF = 3072
CODES = 1024
CODE_DIM = 32
POS = 1024
FRAMES = 16
CLIPS = 2


def draw_code_index(key, part):
    key = jax.random.fold_in(key, 11)
    key_inner, key_order, key_first, key_second, key_where, key_offset = jax.random.split(key, 6)
    dropped = CODES // 8
    inner = 1 + jax.random.permutation(key_inner, CODES - 2).astype(jnp.int32)
    usable = jnp.concatenate([jnp.array([0, CODES - 1], jnp.int32), inner[dropped:]])
    usable = usable[jax.random.permutation(key_order, usable.shape[0])]
    total = CLIPS * FRAMES * POS
    first_rank = jax.random.randint(key_first, (total,), 0, usable.shape[0], dtype=jnp.int32)
    second_rank = jax.random.randint(key_second, (total,), 0, usable.shape[0], dtype=jnp.int32)
    picks = usable[jnp.minimum(first_rank, second_rank)]
    where_zero = jax.random.randint(key_where, (), 0, total, dtype=jnp.int32)
    where_last = (where_zero + 1 + jax.random.randint(key_offset, (), 0, total - 1, dtype=jnp.int32)) % total
    picks = picks.at[where_zero].set(0)
    picks = picks.at[where_last].set(CODES - 1)
    return picks.reshape(CLIPS, FRAMES, POS).astype(jnp.int32)


def levels(own_key, shape, shards, low, largest):
    def one(axis_at, parts):
        steps = jax.random.uniform(jax.random.fold_in(jax.random.fold_in(own_key, 6), axis_at), (parts,), jnp.float32, low / len(shards), largest / len(shards))
        return jnp.repeat(jnp.exp(steps), shape[axis_at] // parts).reshape((-1,) + (1,) * (len(shape) - axis_at - 1))

    level = one(*shards[0])
    for cut in shards[1:]:
        level = level * one(*cut)
    return level


def gaussian(rng, dims, deviation, limit, pieces=(), held_as=jnp.bfloat16):
    level = levels(rng, dims, pieces, -0.22, 0.18) if pieces else 1.0
    values = jax.random.normal(rng, dims, jnp.float32) * deviation * level
    return jnp.minimum(jnp.maximum(values, -limit), limit).astype(held_as)


def setup_inputs(seed: int = 0) -> dict:
    streams_of = jax.random.split(jax.random.key(seed), 13)
    return {
        "frames_in": gaussian(streams_of[0], (CLIPS, FRAMES, POS, D), 1.0, 6.0, ((0, 2), (1, 16))),
        "gain_space": jnp.clip(1.0 + 0.18 * jax.random.normal(streams_of[1], (D,), jnp.float32), 0.1, 1.9),
        "space_proj": gaussian(streams_of[2], (3, D, S_HEADS * HD), D ** -0.5, 0.21875, ((2, 8),)),
        "space_out": gaussian(streams_of[3], (S_HEADS * HD, D), (S_HEADS * HD) ** -0.5, 0.25),
        "gain_time": jnp.clip(1.0 + 0.18 * jax.random.normal(streams_of[4], (D,), jnp.float32), 0.1, 1.9),
        "time_proj": gaussian(streams_of[5], (3, D, D), D ** -0.5, 0.21875),
        "time_out": gaussian(streams_of[6], (D, D), D ** -0.5, 0.21875),
        "gain_mlp": jnp.clip(1.0 + 0.18 * jax.random.normal(streams_of[7], (D,), jnp.float32), 0.1, 1.9),
        "mlp_in": gaussian(streams_of[8], (FF, D), D ** -0.5, 0.21875, ((0, 128),)),
        "mlp_out": gaussian(streams_of[9], (FF, D), FF ** -0.5, 0.109375, ((0, 128),)),
        "code_proj": gaussian(streams_of[10], (D, CODE_DIM), D ** -0.5, 0.21875),
        "code_index": draw_code_index(jax.random.fold_in(streams_of[12], 71), 0),
    }


def layer_norm(values, gain):
    center = lax.optimization_barrier(jnp.mean(values, axis=-1, keepdims=True))
    spread = lax.optimization_barrier(jnp.mean((values - center) ** 2, axis=-1, keepdims=True))
    return (values - center) * lax.rsqrt(spread + 1e-06) * gain

def attend_frame(queries, keys, values, factor):
    positions, heads_n, head_size = queries.shape
    block_rows = math.gcd(positions, 512)
    query_blocks = queries.reshape(positions // block_rows, block_rows, heads_n, head_size)
    keys_wide = keys.astype(jnp.float32)
    values_wide = values.astype(jnp.float32)

    def per_block(query_block):
        scores = jnp.einsum('qhd,khd->hqk', query_block.astype(jnp.float32), keys_wide) * factor
        weights = jax.nn.softmax(scores, axis=-1).astype(jnp.bfloat16)
        return jnp.einsum('hqk,khd->qhd', weights.astype(jnp.float32), values_wide).astype(jnp.bfloat16)
    return lax.map(per_block, query_blocks).reshape(positions, heads_n * head_size)

def attend_time(queries, keys, values, factor):
    frames_n = queries.shape[0]
    scores = jnp.einsum('fnhd,gnhd->nhfg', queries.astype(jnp.float32), keys.astype(jnp.float32)) * factor
    later = lax.broadcasted_iota(jnp.int32, (frames_n, frames_n), 0)
    earlier = lax.broadcasted_iota(jnp.int32, (frames_n, frames_n), 1)
    scores = jnp.where(earlier <= later, scores, -jnp.inf)
    weights = jax.nn.softmax(scores, axis=-1).astype(jnp.bfloat16)
    return jnp.einsum('nhfg,gnhd->fnhd', weights.astype(jnp.float32), values.astype(jnp.float32)).astype(jnp.bfloat16)

def reference(frames_in, gain_space, space_proj, space_out, gain_time, time_proj, time_out, gain_mlp, mlp_in, mlp_out, code_proj, code_index):
    factor = 1.0 / math.sqrt(HD)

    def spatial(frame_tokens):
        normed = layer_norm(frame_tokens.astype(jnp.float32), gain_space).astype(jnp.bfloat16)
        projected = jnp.einsum('pd,sdc->spc', normed.astype(jnp.float32), space_proj.astype(jnp.float32)).astype(jnp.bfloat16)
        projected = projected.reshape(3, POS, S_HEADS, HD)
        heads_out = attend_frame(projected[0], projected[1], projected[2], factor)
        return frame_tokens.astype(jnp.float32) + jnp.dot(heads_out, space_out, preferred_element_type=jnp.float32)
    after_space = lax.map(spatial, frames_in.reshape(CLIPS * FRAMES, POS, D))
    group = 128
    nblocks = POS // group
    grouped = after_space.reshape(CLIPS, FRAMES, nblocks, group, D).transpose(0, 2, 1, 3, 4).reshape(CLIPS * nblocks, FRAMES, group, D)

    def finish(tokens):
        row_count = FRAMES * group
        normed = layer_norm(tokens, gain_time).astype(jnp.bfloat16).reshape(row_count, D)
        projected = jnp.einsum('rd,sdc->src', normed.astype(jnp.float32), time_proj.astype(jnp.float32)).astype(jnp.bfloat16)
        projected = projected.reshape(3, FRAMES, group, T_HEADS, HD)
        heads_out = attend_time(projected[0], projected[1], projected[2], factor).reshape(row_count, D)
        after_time = tokens.reshape(row_count, D) + jnp.dot(heads_out, time_out, preferred_element_type=jnp.float32)
        mlp_act = layer_norm(after_time, gain_mlp).astype(jnp.bfloat16)
        pre_act = jnp.dot(mlp_act, mlp_in.T, preferred_element_type=jnp.float32)
        hidden = jax.nn.gelu(pre_act, approximate=True).astype(jnp.bfloat16)
        after_mlp = after_time + jnp.dot(hidden, mlp_out, preferred_element_type=jnp.float32)
        outputs = after_mlp.astype(jnp.bfloat16)
        code_vec = jnp.dot(outputs, code_proj, preferred_element_type=jnp.float32)
        return (outputs.reshape(FRAMES, group, D), code_vec.reshape(FRAMES, group, CODE_DIM))
    outputs, code_vec = lax.map(finish, grouped)
    block_out = outputs.reshape(CLIPS, nblocks, FRAMES, group, D).transpose(0, 2, 1, 3, 4).reshape(CLIPS, FRAMES, POS, D)
    code_vec = code_vec.reshape(CLIPS, nblocks, FRAMES, group, CODE_DIM).transpose(0, 2, 1, 3, 4).reshape(-1, CODE_DIM)
    flat_index = code_index.reshape(-1).astype(jnp.int32)
    code_sums = jax.ops.segment_sum(code_vec, flat_index, num_segments=CODES)
    code_counts = jax.ops.segment_sum(jnp.ones(flat_index.shape, jnp.float32), flat_index, num_segments=CODES)
    code_means = code_sums / jnp.maximum(code_counts, 1.0)[:, None]
    return (block_out, code_means)
```

```python
import math

import jax
import jax.numpy as jnp
from jax import lax
from jax.experimental import pallas as pl
from jax.experimental.pallas import tpu as pltpu
from jax.sharding import PartitionSpec as P

F32 = jnp.float32
BF16 = jnp.bfloat16
MESH = pl.DeviceIdType.MESH

D = 768
HALF = D // 2
HD = 64
T_HEADS = 12
CODES = 1024
POS = 1024
FRAMES = 16
NX, NY, NZ = 4, 4, 8
SIZE = {"x": NX, "y": NY, "z": NZ}
ORDERS = (("x", "y", "z"), ("y", "z", "x"), ("z", "x", "y"))
UNITS = tuple(SIZE[order[0]] // 2 * 8 for order in ORDERS)


def layer_norm(values, gain):
    center = jnp.mean(values, axis=-1, keepdims=True)
    shifted = values - center
    spread = jnp.mean(shifted * shifted, axis=-1, keepdims=True)
    return shifted * lax.rsqrt(spread + 1e-06) * gain


def nt_dot(a, b):
    return lax.dot_general(a, b, (((1,), (1,)), ((), ())), preferred_element_type=F32)


def gelu(v):
    inner = math.sqrt(2.0 / math.pi) * (v + 0.044715 * (v * v * v))
    return 0.5 * v * (1.0 + jnp.tanh(inner))


def lanes(shape):
    return lax.broadcasted_iota(jnp.int32, shape, len(shape) - 1)


def block_kernel(
    frames_hbm, gs_ref, sproj_hbm, sout_hbm, gt_ref, tproj_hbm, tout_hbm, gm_ref,
    win_ref, wout_ref, cproj_ref, cidx_ref,
    out_ref, means_ref,
    fr, sp, so, tp, to, q_s, k_s, v_s,
    heads_send, heads_recv, rows_send, rows_recv,
    own_parts, first0, first1, first2, w0, w1, w2,
    act_send, act_recv, back_send, back_recv,
    sums_send, sums_recv, tot_all, mean_send, mean_recv,
    load_sem, heads_ss, heads_rs, rows_ss, rows_rs, first_ss, first_rs,
    ring_ss, ring_rs, pair_ss, pair_rs, red_ss, red_rs, tot_ss, tot_rs, fin_ss, fin_rs,
):
    c = lax.axis_index("dp")
    f = lax.axis_index("frame")
    m = lax.axis_index("mp")
    me = {"x": f // NY, "y": f % NY, "z": m}
    group = c * NZ + m

    def at(**moved):
        x = moved.get("x", me["x"])
        y = moved.get("y", me["y"])
        return (c, x * NY + y, moved.get("z", m))

    def frame_peer(k):
        return (c, (f + k) % FRAMES, m)

    def group_peer(k):
        other = (group + k) % 16
        return (other // NZ, f, other % NZ)

    barrier = pltpu.get_barrier_semaphore()

    @pl.loop(1, 16)
    def _(k):
        pl.semaphore_signal(barrier, inc=1, device_id=frame_peer(k), device_id_type=MESH)
        pl.semaphore_signal(barrier, inc=1, device_id=group_peer(k), device_id_type=MESH)

    loads = [pltpu.make_async_copy(sproj_hbm, sp, load_sem.at[0])]
    for i in range(4):
        rows = pl.ds(i * 256, 256)
        loads.append(pltpu.make_async_copy(frames_hbm.at[0, 0, rows], fr.at[rows], load_sem.at[1 + i]))
    loads.append(pltpu.make_async_copy(sout_hbm, so, load_sem.at[5]))
    loads.append(pltpu.make_async_copy(tproj_hbm, tp, load_sem.at[6]))
    loads.append(pltpu.make_async_copy(tout_hbm, to, load_sem.at[7]))
    for load in loads:
        load.start()

    win = win_ref[...].astype(F32)
    wout = wout_ref[...].astype(F32)
    for p in range(3):
        own_parts[p] = jnp.concatenate(
            [win[p * 8 : p * 8 + 8], wout[p * 8 : p * 8 + 8]], axis=0
        ).astype(BF16)
    firsts = (first0, first1, first2)
    gathered = (w0, w1, w2)
    waits = []

    def first_copy(p, k, slot):
        axis = ORDERS[p][0]
        return pltpu.make_async_remote_copy(
            src_ref=own_parts.at[p], dst_ref=firsts[p].at[slot],
            send_sem=first_ss.at[p, k], recv_sem=first_rs.at[p, slot],
            device_id=at(**{axis: (me[axis] + k) % SIZE[axis]}), device_id_type=MESH,
        )

    def first_send(p):
        axis = ORDERS[p][0]
        n = SIZE[axis]
        slot = me[axis] % (n // 2)

        @pl.when(me[axis] // (n // 2) == c)
        def _():
            firsts[p][slot] = own_parts[p]
            for k in range(1, n):
                first_copy(p, k, slot).start()

    def first_wait(p):
        axis = ORDERS[p][0]
        n = SIZE[axis]
        for slot in range(n // 2):
            @pl.when(c * (n // 2) + slot != me[axis])
            def _():
                first_copy(p, 1, slot).wait_recv()
        block = firsts[p][...].astype(F32).reshape(n // 2, 2, 8, D)
        at3, at2 = me[ORDERS[p][2]], me[ORDERS[p][1]]
        for side in range(2):
            gathered[p][at3, at2, side] = block[:, side].reshape(n // 2 * 8, D).astype(BF16)

    def first_done(p):
        axis = ORDERS[p][0]
        n = SIZE[axis]

        @pl.when(me[axis] // (n // 2) == c)
        def _():
            for k in range(1, n):
                first_copy(p, k, 0).wait_send()

    def ring_copy(p, phase, step, way):
        axis = ORDERS[p][phase]
        n = SIZE[axis]
        shift = (n - (step - 1)) if way == 0 else (step - 1)
        index = (me[axis] + shift) % n
        if phase == 1:
            block = gathered[p].at[me[ORDERS[p][2]], index]
            if step == n // 2:
                block = block.at[way]
        else:
            block = gathered[p].at[index]
            if step == n // 2:
                inner = SIZE[ORDERS[p][1]] // 2
                block = block.at[pl.ds(way * inner, inner)]
        to_index = (me[axis] + (1 if way == 0 else n - 1)) % n
        return pltpu.make_async_remote_copy(
            src_ref=block, dst_ref=block,
            send_sem=ring_ss.at[p, phase - 1, step - 1, way],
            recv_sem=ring_rs.at[p, phase - 1, step - 1, way],
            device_id=at(**{axis: to_index}), device_id_type=MESH,
        )

    plans = []
    for p in range(3):
        plan = [(1, s) for s in range(1, SIZE[ORDERS[p][1]] // 2 + 1)]
        plan += [(2, s) for s in range(1, SIZE[ORDERS[p][2]] // 2 + 1)]
        plans.append(plan)
    stage = [0, 0, 0]

    def advance(p):
        at_step = stage[p]
        stage[p] += 1
        if at_step == 0:
            first_send(p)
            return
        if at_step == 1:
            first_wait(p)
        else:
            for way in range(2):
                ring_copy(p, *plans[p][at_step - 2], way).wait_recv()
        if at_step <= len(plans[p]):
            for way in range(2):
                ring_copy(p, *plans[p][at_step - 1], way).start()

    def finish(p):
        while stage[p] < len(plans[p]) + 2:
            advance(p)

    pl.semaphore_wait(barrier, 30)
    for p in (2, 0, 1):
        advance(p)

    loads[0].wait()
    wqkv = jnp.concatenate(
        [sp[0], sp[1], sp[2], jnp.zeros((D, HD), BF16)], axis=1
    )
    gain_space = gs_ref[...].reshape(1, D)
    for i in range(4):
        loads[1 + i].wait()

    @pl.loop(0, 4)
    def _(i):
        rows = pl.ds(pl.multiple_of(i * 256, 256), 256)
        normed = layer_norm(fr[rows, :].astype(F32), gain_space).astype(BF16)
        both = jnp.dot(normed, wqkv, preferred_element_type=F32)
        qk = both[:, :128]
        low = lanes((256, 128)) < HD
        k_s[rows, :] = pltpu.roll(qk, HD, 1).astype(BF16)
        v = both[:, 128:]
        v_s[rows, :] = jnp.where(lanes((256, 128)) == HD, 1.0, v).astype(BF16)
        q = jnp.where(low, qk * (1.0 / math.sqrt(HD)), 0.0).reshape(4, NZ, 8, 128)
        for to_m in range(NZ):
            q_s[to_m, pl.ds(pl.multiple_of(i * 32, 32), 32), :] = (
                q[:, to_m].reshape(32, 128).astype(BF16)
            )

    for p in (0, 1, 2):
        advance(p)

    def heads_copy(shift):
        dest = (m + shift) % NZ
        return pltpu.make_async_remote_copy(
            src_ref=heads_send.at[dest], dst_ref=heads_recv.at[m],
            send_sem=heads_ss.at[shift], recv_sem=heads_rs.at[shift],
            device_id=(c, f, dest), device_id_type=MESH,
        )

    @pl.loop(0, NZ)
    def _(i):
        shift = 4 + ((i + 1) // 2) * (1 - 2 * (i % 2))
        dest = (m + shift) % NZ
        scores = nt_dot(q_s[dest], k_s[...])
        top = jnp.max(scores, axis=-1, keepdims=True)
        weights = jnp.exp(scores - top).astype(BF16)
        mixed = jnp.dot(weights, v_s[...], preferred_element_type=F32)
        mixed = mixed / mixed[:, HD : HD + 1]
        packed = jnp.where(lanes((64, 128)) < HD, mixed[:64], pltpu.roll(mixed[64:], HD, 1))
        heads_send[dest] = packed.astype(BF16)

        @pl.when(shift != 0)
        def _():
            heads_copy(shift).start()

        @pl.when(i == 2)
        def _():
            for p in range(3):
                advance(p)

        @pl.when(i == 5)
        def _():
            for p in range(3):
                advance(p)

    heads_recv[m] = heads_send[m]
    for k in range(1, NZ):
        heads_copy(k).wait_recv()
    advance(1)

    side = lanes((64, 128)) < HD
    upper, lower = [], []
    for i in range(NZ // 2):
        even = heads_recv[2 * i].astype(F32)
        odd = heads_recv[2 * i + 1].astype(F32)
        upper.append(jnp.where(side, even, pltpu.roll(odd, HD, 1)))
        lower.append(jnp.where(side, pltpu.roll(even, HD, 1), odd))
    heads_all = jnp.concatenate(
        [jnp.concatenate(upper, axis=1), jnp.concatenate(lower, axis=1)], axis=0
    ).astype(BF16)
    own = []
    for i in range(FRAMES):
        pair = fr[pl.ds(pl.multiple_of(i * 64 + (m // 2) * 16, 16), 16), :].astype(F32)
        own.append(jnp.where(m % 2 == 0, pair[:8], pair[8:]))
    loads[5].wait()
    after_space = jnp.concatenate(own, axis=0) + jnp.dot(
        heads_all, so[...], preferred_element_type=F32
    )
    split = after_space.reshape(FRAMES, 8, D)
    rows_send[...] = jnp.concatenate([split[:, :, :HALF], split[:, :, HALF:]], axis=1).astype(BF16)

    def rows_copy(k):
        dest = (f + k) % FRAMES
        return pltpu.make_async_remote_copy(
            src_ref=rows_send.at[dest], dst_ref=rows_recv.at[f],
            send_sem=rows_ss.at[k], recv_sem=rows_rs.at[k],
            device_id=(c, dest, m), device_id_type=MESH,
        )

    @pl.loop(1, FRAMES)
    def _(k):
        rows_copy(k).start()

    rows_recv[f] = rows_send[f]
    advance(1)
    advance(0)

    @pl.loop(1, FRAMES)
    def _(k):
        rows_copy(k).wait_recv()

    arrived = rows_recv[...].astype(F32)
    after_space = jnp.concatenate([arrived[:, :8], arrived[:, 8:]], axis=2).reshape(128, D)
    loads[6].wait()
    loads[7].wait()
    time_in = layer_norm(after_space, gt_ref[...].reshape(1, D)).astype(BF16)
    tq = jnp.dot(time_in, tp[0], preferred_element_type=F32) * (1.0 / math.sqrt(HD))
    tk = jnp.dot(time_in, tp[1], preferred_element_type=F32).astype(BF16)
    tv = jnp.dot(time_in, tp[2], preferred_element_type=F32).astype(BF16)
    row = lax.broadcasted_iota(jnp.int32, (128, 128), 0)
    col = lax.broadcasted_iota(jnp.int32, (128, 128), 1)
    seen = (row % 8 == col % 8) & (col // 8 <= row // 8)
    low = col < HD
    pieces = []
    for i in range(T_HEADS // 2):
        cut = slice(i * 128, i * 128 + 128)
        both = []
        for own_half in (low, jnp.logical_not(low)):
            scores = nt_dot(jnp.where(own_half, tq[:, cut], 0.0).astype(BF16), tk[:, cut])
            scores = jnp.where(seen, scores, -jnp.inf)
            weights = jnp.exp(scores - jnp.max(scores, axis=-1, keepdims=True))
            weights = weights / jnp.sum(weights, axis=-1, keepdims=True)
            both.append(jnp.dot(weights.astype(BF16), tv[:, cut], preferred_element_type=F32))
        pieces.append(jnp.where(low, both[0], both[1]).astype(BF16))
    advance(0)
    advance(2)
    time_heads = jnp.concatenate(pieces, axis=1)
    after_time = after_space + jnp.dot(time_heads, to[...], preferred_element_type=F32)
    act_send[...] = layer_norm(after_time, gm_ref[...].reshape(1, D)).astype(BF16)

    partner = (1 - c, f, m)
    act_copy = pltpu.make_async_remote_copy(
        src_ref=act_send, dst_ref=act_recv, send_sem=pair_ss.at[0], recv_sem=pair_rs.at[0],
        device_id=partner, device_id_type=MESH,
    )
    act_copy.start()
    for p in (2, 0, 1):
        finish(p)
    act_copy.wait_recv()
    act = jnp.concatenate([act_recv[...], act_send[...]], axis=0)
    partial = jnp.zeros((256, D), F32)
    for p in (2, 0, 1):
        n3 = gathered[p].shape[0]
        for lo in range(0, n3, n3 // 2):
            part = gathered[p][lo : lo + n3 // 2]
            hidden = gelu(nt_dot(act, part[:, :, 0].reshape(256, D))).astype(BF16)
            partial += jnp.dot(hidden, part[:, :, 1].reshape(256, D), preferred_element_type=F32)
    back_send[...] = partial[:128]
    back_copy = pltpu.make_async_remote_copy(
        src_ref=back_send, dst_ref=back_recv, send_sem=pair_ss.at[1], recv_sem=pair_rs.at[1],
        device_id=partner, device_id_type=MESH,
    )
    back_copy.start()
    after_time = after_time + partial[128:]
    codes = jnp.broadcast_to(cidx_ref[0][:, None, :], (FRAMES, 8, 8)).reshape(128, 8)
    diagonal = lax.broadcasted_iota(jnp.int32, (128, 8), 0) % 8 == lanes((128, 8))
    codes = jnp.sum(jnp.where(diagonal, codes, 0), axis=1, keepdims=True)
    onehot = (codes == lanes((128, CODES))).astype(F32).astype(BF16)
    code_proj = cproj_ref[...].astype(F32).T.astype(BF16)
    back_copy.wait_recv()
    outputs = (after_time + back_recv[...]).astype(BF16)
    out_ref[0] = outputs.astype(F32).reshape(FRAMES, 8, D).astype(BF16)

    vecs = nt_dot(code_proj, outputs)
    high = vecs.astype(BF16)
    rest = (vecs - high.astype(F32)).astype(BF16)
    ones = jnp.ones((8, 128), F32)
    zeros = jnp.zeros((8, 128), F32)
    high32, rest32 = high.astype(F32), rest.astype(F32)
    left = jnp.concatenate(
        [high32[:16], ones, high32[16:], ones, rest32[:16], zeros, rest32[16:], zeros], axis=0
    ).astype(BF16)
    sums = jnp.dot(left, onehot, preferred_element_type=F32)
    sums = sums[:48] + sums[48:]
    for to_c in range(2):
        for to_m in range(NZ):
            sums_send[to_c * NZ + to_m] = sums[
                to_c * 24 : to_c * 24 + 24, to_m * 128 : to_m * 128 + 128
            ]

    def group_copy(k, src, dst, send_sem, recv_sem):
        return pltpu.make_async_remote_copy(
            src_ref=src, dst_ref=dst, send_sem=send_sem.at[k], recv_sem=recv_sem.at[k],
            device_id=group_peer(k), device_id_type=MESH,
        )

    def sums_copy(k):
        return group_copy(k, sums_send.at[(group + k) % 16], sums_recv.at[k], red_ss, red_rs)

    def tot_copy(k):
        return pltpu.make_async_remote_copy(
            src_ref=tot_all.at[f], dst_ref=tot_all.at[f], send_sem=tot_ss.at[k],
            recv_sem=tot_rs.at[k], device_id=frame_peer(k), device_id_type=MESH,
        )

    def mean_copy(k):
        return group_copy(k, mean_send, mean_recv.at[group], fin_ss, fin_rs)

    @pl.loop(1, 16)
    def _(k):
        sums_copy(k).start()

    @pl.loop(1, 16)
    def _(k):
        sums_copy(k).wait_recv()

    total = sums_send[group]
    for k in range(1, 16):
        total += sums_recv[k]
    tot_all[f] = total

    @pl.loop(1, 16)
    def _(k):
        tot_copy(k).start()

    @pl.loop(1, 16)
    def _(k):
        tot_copy(k).wait_recv()

    total = tot_all[0]
    for k in range(1, 16):
        total += tot_all[k]
    means = total[:16] / jnp.maximum(total[16:17], 1.0)
    mean_send[...] = means
    mean_recv[group] = means

    @pl.loop(1, 16)
    def _(k):
        mean_copy(k).start()

    for p in range(3):
        first_done(p)
        for phase, step in plans[p]:
            for way in range(2):
                ring_copy(p, phase, step, way).wait_send()
    for k in range(1, NZ):
        heads_copy(k).wait_send()
    act_copy.wait_send()
    back_copy.wait_send()

    @pl.loop(1, 16)
    def _(k):
        rows_copy(k).wait_send()
        sums_copy(k).wait_send()
        tot_copy(k).wait_send()
        mean_copy(k).wait_send()
        mean_copy(k).wait_recv()

    for g in range(16):
        cut = slice(g % NZ * 128, g % NZ * 128 + 128)
        means_ref[g // NZ * 16 : g // NZ * 16 + 16, cut] = mean_recv[g]


def shards(*args):
    vmem = pl.BlockSpec(memory_space=pltpu.VMEM)
    hbm = pl.BlockSpec(memory_space=pltpu.HBM)
    dma = pltpu.SemaphoreType.DMA
    scratch = [
        pltpu.VMEM((POS, D), BF16),
        pltpu.VMEM((3, D, HD), BF16),
        pltpu.VMEM((512, D), BF16),
        pltpu.VMEM((3, D, D), BF16),
        pltpu.VMEM((D, D), BF16),
        pltpu.VMEM((NZ, 128, 128), BF16),
        pltpu.VMEM((POS, 128), BF16),
        pltpu.VMEM((POS, 128), BF16),
        pltpu.VMEM((NZ, 64, 128), BF16),
        pltpu.VMEM((NZ, 64, 128), BF16),
        pltpu.VMEM((FRAMES, 16, HALF), BF16),
        pltpu.VMEM((FRAMES, 16, HALF), BF16),
        pltpu.VMEM((3, 16, D), BF16),
    ]
    scratch += [pltpu.VMEM((SIZE[order[0]] // 2, 16, D), BF16) for order in ORDERS]
    scratch += [
        pltpu.VMEM((SIZE[order[2]], SIZE[order[1]], 2, units, D), BF16)
        for order, units in zip(ORDERS, UNITS)
    ]
    scratch += [
        pltpu.VMEM((128, D), BF16),
        pltpu.VMEM((128, D), BF16),
        pltpu.VMEM((128, D), F32),
        pltpu.VMEM((128, D), F32),
        pltpu.VMEM((16, 24, 128), F32),
        pltpu.VMEM((16, 24, 128), F32),
        pltpu.VMEM((FRAMES, 24, 128), F32),
        pltpu.VMEM((16, 128), F32),
        pltpu.VMEM((16, 16, 128), F32),
    ]
    scratch += [
        dma((8,)),
        dma((NZ,)), dma((NZ,)),
        dma((FRAMES,)), dma((FRAMES,)),
        dma((3, NZ)), dma((3, NZ)),
        dma((3, 2, 4, 2)), dma((3, 2, 4, 2)),
        dma((2,)), dma((2,)),
        dma((16,)), dma((16,)),
        dma((16,)), dma((16,)),
        dma((16,)), dma((16,)),
    ]
    block_out, means = pl.pallas_call(
        block_kernel,
        out_shape=(
            jax.ShapeDtypeStruct((1, FRAMES, 8, D), BF16),
            jax.ShapeDtypeStruct((32, CODES), F32),
        ),
        in_specs=[hbm, vmem, hbm, hbm, vmem, hbm, hbm, vmem, vmem, vmem, vmem, vmem],
        out_specs=(vmem, vmem),
        scratch_shapes=scratch,
        compiler_params=pltpu.CompilerParams(
            collective_id=0, has_side_effects=True, vmem_limit_bytes=48 * 1024 * 1024
        ),
    )(*args)
    return block_out, means.T


def solution(mesh):
    placed = (
        P("dp", "frame", None, None),
        P(),
        P(None, None, "mp"),
        P(),
        P(),
        P(),
        P(),
        P(),
        P(("frame", "mp"), None),
        P(("frame", "mp"), None),
        P(),
        P("dp", None, ("frame", "mp")),
    )
    return jax.shard_map(
        shards,
        mesh=mesh,
        in_specs=placed,
        out_specs=(P("dp", None, ("frame", "mp"), None), P()),
        check_vma=False,
    )
```

```python
import math

import jax
import jax.numpy as jnp
from jax import lax
from jax.experimental import pallas as pl
from jax.experimental.pallas import tpu as pltpu
from jax.sharding import PartitionSpec as P

F32 = jnp.float32
BF16 = jnp.bfloat16
MESH = pl.DeviceIdType.MESH

D = 768
HALF = D // 2
HD = 64
T_HEADS = 12
CODES = 1024
POS = 1024
FRAMES = 16
NX, NY, NZ = 4, 4, 8
SIZE = {"x": NX, "y": NY, "z": NZ}
ORDERS = (("x", "y", "z"), ("z", "y", "x"), ("z", "x", "y"))
UNITS = tuple(SIZE[order[0]] // 2 * 8 for order in ORDERS)
EVENTS = (
    (0, 0), (1, 0), (0, 1, 1), (2, 0), (0, 1, 3), (0, 1, 2),
    (0, 2, 1, 0), (1, 2, 1, 0), (1, 1, 1),
    (0, 2, 1, 1), (2, 1, 1), (1, 1, 3), (1, 1, 2), (0, 2, 1, 3),
    (0, 2, 1, 2), (2, 1, 3), (2, 1, 2), (2, 2, 1, 0),
    (0, 2, 2, 0), (0, 2, 2, 1), (0, 2, 2, 3), (1, 2, 2, 0),
    (0, 2, 2, 2), (2, 2, 1, 1), (0, 2, 3, 0), (1, 2, 1, 1),
    (0, 2, 3, 1), (2, 2, 1, 3), (0, 2, 3, 3), (1, 2, 1, 3),
    (0, 2, 3, 2), (2, 2, 1, 2), (1, 2, 1, 2),
    (2, 2, 2, 0), (0, 2, 4, 0), (0, 2, 4, 1), (1, 2, 2, 1), (2, 2, 2, 1),
    (0, 2, 4, 3), (0, 2, 4, 2), (1, 2, 2, 3), (2, 2, 2, 3), (1, 2, 2, 2), (2, 2, 2, 2),
)


def layer_norm(values, gain):
    center = jnp.mean(values, axis=-1, keepdims=True)
    shifted = values - center
    spread = jnp.mean(shifted * shifted, axis=-1, keepdims=True)
    return shifted * lax.rsqrt(spread + 1e-06) * gain


def nt_dot(a, b):
    return lax.dot_general(a, b, (((1,), (1,)), ((), ())), preferred_element_type=F32)


def gelu(v):
    inner = math.sqrt(2.0 / math.pi) * (v + 0.044715 * (v * v * v))
    return 0.5 * v * (1.0 + jnp.tanh(inner))


def lanes(shape):
    return lax.broadcasted_iota(jnp.int32, shape, len(shape) - 1)


def block_kernel(
    frames_hbm, gs_hbm, sproj_hbm, sout_hbm, gt_hbm, tproj_hbm, tout_hbm, gm_hbm,
    win_hbm, wout_hbm, cproj_hbm, cidx_hbm,
    out_hbm, means_ref,
    fr, gs_ref, sp, so, gt_ref, tp, to, gm_ref, win_ref, wout_ref, cproj_ref, cidx_ref,
    q_s, k_s, v_s,
    heads_send, heads_recv, rows_send, rows_recv,
    own_parts, first0, first1, first2, w0, w1, w2,
    act_send, act_recv, back_send, back_recv,
    out_s, sums_send, sums_recv, red_send, red_recv, tot_all, mean_send, mean_recv,
    load_sem, heads_ss, heads_rs, rows_ss, rows_rs, first_ss, first_rs,
    second_ss, second_rs,    ring_ss, ring_rs, pair_ss, pair_rs, red_ss, red_rs, tot_ss, tot_rs, fin_ss, fin_rs,
):
    c = lax.axis_index("dp")
    f = lax.axis_index("frame")
    m = lax.axis_index("mp")
    me = {"x": f // NY, "y": f % NY, "z": m}
    group = c * NZ + m

    def at(**moved):
        x = moved.get("x", me["x"])
        y = moved.get("y", me["y"])
        return (c, x * NY + y, moved.get("z", m))

    def frame_peer(k):
        return (c, (f + k) % FRAMES, m)

    def group_peer(k):
        other = (group + k) % 16
        return (other // NZ, f, other % NZ)

    barrier = pltpu.get_barrier_semaphore()

    @pl.loop(1, 16)
    def _(k):
        pl.semaphore_signal(barrier, inc=1, device_id=frame_peer(k), device_id_type=MESH)
        pl.semaphore_signal(barrier, inc=1, device_id=group_peer(k), device_id_type=MESH)

    loads = {}
    for name, src, dst in (
        ("win", win_hbm, win_ref), ("wout", wout_hbm, wout_ref),
        ("gs", gs_hbm, gs_ref), ("sp", sproj_hbm, sp), ("fr", frames_hbm.at[0, 0], fr),
        ("so", sout_hbm, so), ("gt", gt_hbm, gt_ref), ("tp", tproj_hbm, tp),
        ("to", tout_hbm, to), ("gm", gm_hbm, gm_ref),
        ("cproj", cproj_hbm, cproj_ref), ("cidx", cidx_hbm, cidx_ref),
    ):
        loads[name] = pltpu.make_async_copy(src, dst, load_sem.at[len(loads)])
        loads[name].start()
    loads["win"].wait()
    loads["wout"].wait()

    win = win_ref[...].astype(F32)
    wout = wout_ref[...].astype(F32)
    for p in range(3):
        own_parts[p] = jnp.concatenate(
            [win[p * 8 : p * 8 + 8], wout[p * 8 : p * 8 + 8]], axis=0
        ).astype(BF16)
    firsts = (first0, first1, first2)
    gathered = (w0, w1, w2)

    def first_copy(p, k, slot):
        axis = ORDERS[p][0]
        return pltpu.make_async_remote_copy(
            src_ref=own_parts.at[p], dst_ref=firsts[p].at[slot],
            send_sem=first_ss.at[p, k], recv_sem=first_rs.at[p, slot],
            device_id=at(**{axis: (me[axis] + k) % SIZE[axis]}), device_id_type=MESH,
        )

    def first_send(p):
        axis = ORDERS[p][0]
        n = SIZE[axis]
        slot = me[axis] % (n // 2)

        @pl.when(me[axis] // (n // 2) == c)
        def _():
            firsts[p][slot] = own_parts[p]
            for k in range(1, n):
                first_copy(p, k, slot).start()

    def first_wait(p):
        axis = ORDERS[p][0]
        n = SIZE[axis]
        for slot in range(n // 2):
            @pl.when(c * (n // 2) + slot != me[axis])
            def _():
                first_copy(p, 1, slot).wait_recv()
        block = firsts[p][...].astype(F32).reshape(n // 2, 2, 8, D)
        at3, at2 = me[ORDERS[p][2]], me[ORDERS[p][1]]
        for side in range(2):
            gathered[p][at3, at2, side] = block[:, side].reshape(n // 2 * 8, D).astype(BF16)

    def first_done(p):
        axis = ORDERS[p][0]
        n = SIZE[axis]

        @pl.when(me[axis] // (n // 2) == c)
        def _():
            for k in range(1, n):
                first_copy(p, k, 0).wait_send()

    def second_copy(p, k):
        _, axis, last = ORDERS[p]
        block = gathered[p].at[me[last], me[axis]]
        return pltpu.make_async_remote_copy(
            src_ref=block, dst_ref=block,
            send_sem=second_ss.at[p, k], recv_sem=second_rs.at[p, k],
            device_id=at(**{axis: (me[axis] + k) % SIZE[axis]}), device_id_type=MESH,
        )

    def ring_copy(p, step, sub, way):
        _, inner, axis = ORDERS[p]
        n = SIZE[axis]
        shift = (n - (step - 1)) if way == 0 else (step - 1)
        block = gathered[p].at[
            (me[axis] + shift) % n, (me[inner] + SIZE[inner] - sub) % SIZE[inner]
        ]
        if step == n // 2:
            block = block.at[way]
        return pltpu.make_async_remote_copy(
            src_ref=block, dst_ref=block,
            send_sem=ring_ss.at[p, step - 1, sub, way],
            recv_sem=ring_rs.at[p, step - 1, sub, way],
            device_id=at(**{axis: (me[axis] + (1 if way == 0 else n - 1)) % n}),
            device_id_type=MESH,
        )

    def ring_send(p, step, sub):
        if step <= SIZE[ORDERS[p][2]] // 2:
            for way in range(2):
                ring_copy(p, step, sub, way).start()

    todo = list(EVENTS)

    def gather(count):
        for event in todo[:count]:
            p = event[0]
            if event[1] == 0:
                first_wait(p)
                for k in (1, 3, 2):
                    second_copy(p, k).start()
                ring_send(p, 1, 0)
            elif event[1] == 1:
                second_copy(p, event[2]).wait_recv()
                ring_send(p, 1, event[2])
            else:
                for way in range(2):
                    ring_copy(p, event[2], event[3], way).wait_recv()
                ring_send(p, event[2] + 1, event[3])
        del todo[:count]

    def gather_sent():
        for p in range(3):
            first_done(p)
            for k in range(1, 4):
                second_copy(p, k).wait_send()
            for step in range(1, SIZE[ORDERS[p][2]] // 2 + 1):
                for sub in range(4):
                    for way in range(2):
                        ring_copy(p, step, sub, way).wait_send()

    for name in ("gs", "sp", "fr"):
        loads[name].wait()
    wqkv = jnp.concatenate([sp[...].reshape(3 * HD, D), jnp.zeros((HD, D), BF16)], axis=0)
    gain_space = gs_ref[...].reshape(1, D)

    @pl.loop(0, 4)
    def _(i):
        rows = pl.ds(pl.multiple_of(i * 256, 256), 256)
        normed = layer_norm(fr[rows, :].astype(F32), gain_space).astype(BF16)
        both = nt_dot(normed, wqkv)
        qk = both[:, :128]
        low = lanes((256, 128)) < HD
        k_s[rows, :] = pltpu.roll(qk, HD, 1).astype(BF16)
        v = both[:, 128:]
        v_s[rows, :] = jnp.where(lanes((256, 128)) == HD, 1.0, v).astype(BF16)
        q = jnp.where(low, qk * (1.0 / math.sqrt(HD)), 0.0).reshape(4, NZ, 8, 128)
        for to_m in range(NZ):
            q_s[to_m, pl.ds(pl.multiple_of(i * 32, 32), 32), :] = (
                q[:, to_m].reshape(32, 128).astype(BF16)
            )

    pl.semaphore_wait(barrier, 30)
    for p in range(3):
        first_send(p)

    def heads_copy(shift):
        dest = (m + shift) % NZ
        return pltpu.make_async_remote_copy(
            src_ref=heads_send.at[dest], dst_ref=heads_recv.at[m],
            send_sem=heads_ss.at[shift], recv_sem=heads_rs.at[shift],
            device_id=(c, f, dest), device_id_type=MESH,
        )

    @pl.loop(0, NZ)
    def _(i):
        shift = 4 + ((i + 1) // 2) * (1 - 2 * (i % 2))
        dest = (m + shift) % NZ
        scores = nt_dot(q_s[dest], k_s[...])
        top = jnp.max(scores, axis=-1, keepdims=True)
        weights = jnp.exp(scores - top).astype(BF16)
        mixed = jnp.dot(weights, v_s[...], preferred_element_type=F32)
        mixed = mixed / mixed[:, HD : HD + 1]
        packed = jnp.where(lanes((64, 128)) < HD, mixed[:64], pltpu.roll(mixed[64:], HD, 1))
        heads_send[dest] = packed.astype(BF16)

        @pl.when(shift != 0)
        def _():
            heads_copy(shift).start()

        @pl.when(i == 5)
        def _():
            gather(1)

        @pl.when(i == 7)
        def _():
            gather(1)

    heads_recv[m] = heads_send[m]
    gather(4)
    for k in range(1, NZ):
        heads_copy(k).wait_recv()

    side = lanes((64, 128)) < HD
    upper, lower = [], []
    for i in range(NZ // 2):
        even = heads_recv[2 * i].astype(F32)
        odd = heads_recv[2 * i + 1].astype(F32)
        upper.append(jnp.where(side, even, pltpu.roll(odd, HD, 1)))
        lower.append(jnp.where(side, pltpu.roll(even, HD, 1), odd))
    heads_all = jnp.concatenate(
        [jnp.concatenate(upper, axis=1), jnp.concatenate(lower, axis=1)], axis=0
    ).astype(BF16)
    own = []
    for i in range(FRAMES):
        pair = fr[pl.ds(pl.multiple_of(i * 64 + (m // 2) * 16, 16), 16), :].astype(F32)
        own.append(jnp.where(m % 2 == 0, pair[:8], pair[8:]))
    loads["so"].wait()
    after_space = jnp.concatenate(own, axis=0) + jnp.dot(
        heads_all, so[...], preferred_element_type=F32
    )
    split = after_space.reshape(FRAMES, 8, D)
    rows_send[...] = jnp.concatenate([split[:, :, :HALF], split[:, :, HALF:]], axis=1).astype(BF16)

    def rows_copy(k):
        dest = (f + k) % FRAMES
        return pltpu.make_async_remote_copy(
            src_ref=rows_send.at[dest], dst_ref=rows_recv.at[f],
            send_sem=rows_ss.at[k], recv_sem=rows_rs.at[k],
            device_id=(c, dest, m), device_id_type=MESH,
        )

    @pl.loop(1, FRAMES)
    def _(k):
        rows_copy(k).start()

    rows_recv[f] = rows_send[f]
    gather(12)

    @pl.loop(1, FRAMES)
    def _(k):
        rows_copy(k).wait_recv()

    arrived = rows_recv[...].astype(F32)
    after_space = jnp.concatenate([arrived[:, :8], arrived[:, 8:]], axis=2).reshape(128, D)
    for name in ("gt", "tp", "to", "gm", "cproj", "cidx"):
        loads[name].wait()
    time_in = layer_norm(after_space, gt_ref[...].reshape(1, D)).astype(BF16)
    tq = jnp.dot(time_in, tp[0], preferred_element_type=F32) * (1.0 / math.sqrt(HD))
    tk = jnp.dot(time_in, tp[1], preferred_element_type=F32).astype(BF16)
    tv = jnp.dot(time_in, tp[2], preferred_element_type=F32).astype(BF16)
    gather(1)
    row = lax.broadcasted_iota(jnp.int32, (128, 128), 0)
    col = lax.broadcasted_iota(jnp.int32, (128, 128), 1)
    seen = (row % 8 == col % 8) & (col // 8 <= row // 8)
    low = col < HD
    pieces = []
    for i in range(T_HEADS // 2):
        cut = slice(i * 128, i * 128 + 128)
        both = []
        for own_half in (low, jnp.logical_not(low)):
            scores = nt_dot(jnp.where(own_half, tq[:, cut], 0.0).astype(BF16), tk[:, cut])
            scores = jnp.where(seen, scores, -jnp.inf)
            weights = jnp.exp(scores - jnp.max(scores, axis=-1, keepdims=True))
            weights = weights / jnp.sum(weights, axis=-1, keepdims=True)
            both.append(jnp.dot(weights.astype(BF16), tv[:, cut], preferred_element_type=F32))
        pieces.append(jnp.where(low, both[0], both[1]).astype(BF16))
        gather((1, 2, 0, 2, 0, 2)[i])
    time_heads = jnp.concatenate(pieces, axis=1)
    after_time = after_space + jnp.dot(time_heads, to[...], preferred_element_type=F32)
    gather(2)
    act_send[...] = layer_norm(after_time, gm_ref[...].reshape(1, D)).astype(BF16)

    partner = (1 - c, f, m)
    act_copy = pltpu.make_async_remote_copy(
        src_ref=act_send, dst_ref=act_recv, send_sem=pair_ss.at[0], recv_sem=pair_rs.at[0],
        device_id=partner, device_id_type=MESH,
    )
    act_copy.start()
    gather(7)
    act_copy.wait_recv()
    act = jnp.concatenate([act_recv[...], act_send[...]], axis=0)
    partial = jnp.zeros((256, D), F32)
    for late in range(2):
        for p in (1, 0, 2):
            at3 = me[ORDERS[p][2]]
            if p == 0:
                steps = (6, 3, 5, 4) if late else (0, 1, 7, 2)
            else:
                steps = (3, 2) if late else (0, 1)
            part = [gathered[p][(at3 + step) % SIZE[ORDERS[p][2]]] for step in steps]
            w_in = jnp.concatenate([block[:, 0].reshape(-1, D) for block in part], axis=0)
            w_out = jnp.concatenate([block[:, 1].reshape(-1, D) for block in part], axis=0)
            hidden = gelu(nt_dot(act, w_in)).astype(BF16)
            partial += jnp.dot(hidden, w_out, preferred_element_type=F32)
        gather(len(todo))
    back_send[...] = partial[:128]
    back_copy = pltpu.make_async_remote_copy(
        src_ref=back_send, dst_ref=back_recv, send_sem=pair_ss.at[1], recv_sem=pair_rs.at[1],
        device_id=partner, device_id_type=MESH,
    )
    back_copy.start()
    after_time = after_time + partial[128:]
    codes = jnp.broadcast_to(cidx_ref[...], (FRAMES, 8, FRAMES)).reshape(128, FRAMES)
    diagonal = lax.broadcasted_iota(jnp.int32, (128, FRAMES), 0) // 8 == lanes((128, FRAMES))
    codes = jnp.sum(jnp.where(diagonal, codes, 0), axis=1, keepdims=True)
    onehot = (codes == lanes((128, CODES))).astype(F32).astype(BF16)
    back_copy.wait_recv()
    outputs = (after_time + back_recv[...]).astype(BF16)
    out_s[0] = outputs.astype(F32).reshape(FRAMES, 8, D).astype(BF16)
    out_copy = pltpu.make_async_copy(out_s, out_hbm, load_sem.at[0])
    out_copy.start()

    vecs = nt_dot(cproj_ref[...], outputs)
    high = vecs.astype(BF16)
    rest = (vecs - high.astype(F32)).astype(BF16)
    left = jnp.concatenate([high, rest, jnp.ones((16, 128), BF16)], axis=0)
    sums = jnp.dot(left, onehot, preferred_element_type=F32)
    counts = sums[64:72]
    sums = sums[:32] + sums[32:64]
    for to_c in range(2):
        for to_m in range(NZ):
            cut = slice(to_m * 128, to_m * 128 + 128)
            sums_send[to_c, to_m] = jnp.concatenate(
                [sums[to_c * 16 : to_c * 16 + 16, cut], counts[:, cut]], axis=0
            )
    sums_copy = pltpu.make_async_remote_copy(
        src_ref=sums_send.at[1 - c], dst_ref=sums_recv, send_sem=pair_ss.at[2],
        recv_sem=pair_rs.at[2], device_id=partner, device_id_type=MESH,
    )
    sums_copy.start()

    def coded(values):
        many = values[..., 16:24, :]
        upper = jnp.floor(many * (1.0 / 256.0))
        return jnp.concatenate(
            [values[..., :16, :], many - 256.0 * upper, upper], axis=-2
        ).astype(BF16)

    def decoded(values):
        values = values.astype(F32)
        return jnp.concatenate(
            [values[..., :16, :], values[..., 16:24, :] + 256.0 * values[..., 24:, :]], axis=-2
        )

    def red_copy(k):
        dest = (m + k) % NZ
        return pltpu.make_async_remote_copy(
            src_ref=red_send.at[dest], dst_ref=red_recv.at[k], send_sem=red_ss.at[k],
            recv_sem=red_rs.at[k], device_id=(c, f, dest), device_id_type=MESH,
        )

    def tot_copy(k):
        return pltpu.make_async_remote_copy(
            src_ref=tot_all.at[f], dst_ref=tot_all.at[f], send_sem=tot_ss.at[k],
            recv_sem=tot_rs.at[k], device_id=frame_peer(k), device_id_type=MESH,
        )

    def mean_copy(k):
        return pltpu.make_async_remote_copy(
            src_ref=mean_send, dst_ref=mean_recv.at[group], send_sem=fin_ss.at[k],
            recv_sem=fin_rs.at[k], device_id=group_peer(k), device_id_type=MESH,
        )

    sums_copy.wait_recv()
    red_send[...] = coded(sums_send[c] + sums_recv[...])
    for k in (4, 3, 5, 2, 6, 1, 7):
        red_copy(k).start()
    gather_sent()
    red_recv[0] = red_send[m]
    for k in range(1, NZ):
        red_copy(k).wait_recv()
    tot_all[f] = coded(jnp.sum(decoded(red_recv[...]), axis=0))

    @pl.loop(1, 16)
    def _(k):
        tot_copy(k).start()

    for k in range(1, NZ):
        heads_copy(k).wait_send()
        red_copy(k).wait_send()
    act_copy.wait_send()
    back_copy.wait_send()
    sums_copy.wait_send()

    @pl.loop(1, 16)
    def _(k):
        rows_copy(k).wait_send()

    @pl.loop(1, 16)
    def _(k):
        tot_copy(k).wait_recv()

    total = jnp.sum(decoded(tot_all[...]), axis=0)
    means = (total[:16] / jnp.maximum(total[16:17], 1.0)).astype(BF16)
    mean_send[...] = means
    mean_recv[group] = means

    @pl.loop(1, 16)
    def _(k):
        mean_copy(k).start()

    @pl.loop(1, 16)
    def _(k):
        tot_copy(k).wait_send()
        mean_copy(k).wait_send()

    out_copy.wait()

    @pl.loop(1, 16)
    def _(k):
        mean_copy(k).wait_recv()

    for g in range(16):
        cut = slice(g % NZ * 128, g % NZ * 128 + 128)
        means_ref[g // NZ * 16 : g // NZ * 16 + 16, cut] = mean_recv[g].astype(F32)


def shards(*args):
    args = list(args)
    args[2] = args[2].swapaxes(1, 2)
    args[10] = args[10].T
    args[11] = args[11].swapaxes(1, 2)
    vmem = pl.BlockSpec(memory_space=pltpu.VMEM)
    hbm = pl.BlockSpec(memory_space=pltpu.HBM)
    dma = pltpu.SemaphoreType.DMA
    scratch = [
        pltpu.VMEM((POS, D), BF16),
        pltpu.VMEM((D,), F32),
        pltpu.VMEM((3, HD, D), BF16),
        pltpu.VMEM((512, D), BF16),
        pltpu.VMEM((D,), F32),
        pltpu.VMEM((3, D, D), BF16),
        pltpu.VMEM((D, D), BF16),
        pltpu.VMEM((D,), F32),
        pltpu.VMEM((24, D), BF16),
        pltpu.VMEM((24, D), BF16),
        pltpu.VMEM((32, D), BF16),
        pltpu.VMEM((1, 8, FRAMES), jnp.int32),
        pltpu.VMEM((NZ, 128, 128), BF16),
        pltpu.VMEM((POS, 128), BF16),
        pltpu.VMEM((POS, 128), BF16),
        pltpu.VMEM((NZ, 64, 128), BF16),
        pltpu.VMEM((NZ, 64, 128), BF16),
        pltpu.VMEM((FRAMES, 16, HALF), BF16),
        pltpu.VMEM((FRAMES, 16, HALF), BF16),
        pltpu.VMEM((3, 16, D), BF16),
    ]
    scratch += [pltpu.VMEM((SIZE[order[0]] // 2, 16, D), BF16) for order in ORDERS]
    scratch += [
        pltpu.VMEM((SIZE[order[2]], SIZE[order[1]], 2, units, D), BF16)
        for order, units in zip(ORDERS, UNITS)
    ]
    scratch += [
        pltpu.VMEM((128, D), BF16),
        pltpu.VMEM((128, D), BF16),
        pltpu.VMEM((128, D), F32),
        pltpu.VMEM((128, D), F32),
        pltpu.VMEM((1, FRAMES, 8, D), BF16),
        pltpu.VMEM((2, NZ, 24, 128), F32),
        pltpu.VMEM((NZ, 24, 128), F32),
        pltpu.VMEM((NZ, 32, 128), BF16),
        pltpu.VMEM((NZ, 32, 128), BF16),
        pltpu.VMEM((FRAMES, 32, 128), BF16),
        pltpu.VMEM((16, 128), BF16),
        pltpu.VMEM((16, 16, 128), BF16),
    ]
    scratch += [
        dma((12,)),
        dma((NZ,)), dma((NZ,)),
        dma((FRAMES,)), dma((FRAMES,)),
        dma((3, NZ)), dma((3, NZ)),
        dma((3, 4)), dma((3, 4)),
        dma((3, 4, 4, 2)), dma((3, 4, 4, 2)),
        dma((3,)), dma((3,)),
        dma((NZ,)), dma((NZ,)),
        dma((16,)), dma((16,)),
        dma((16,)), dma((16,)),
    ]
    block_out, means = pl.pallas_call(
        block_kernel,
        out_shape=(
            jax.ShapeDtypeStruct((1, FRAMES, 8, D), BF16),
            jax.ShapeDtypeStruct((32, CODES), F32),
        ),
        in_specs=[hbm] * 12,
        out_specs=(hbm, vmem),
        scratch_shapes=scratch,
        compiler_params=pltpu.CompilerParams(
            collective_id=0, has_side_effects=True, vmem_limit_bytes=60 * 1024 * 1024
        ),
    )(*args)
    return block_out, means.T


def solution(mesh):
    placed = (
        P("dp", "frame", None, None),
        P(),
        P(None, None, "mp"),
        P(),
        P(),
        P(),
        P(),
        P(),
        P(("frame", "mp"), None),
        P(("frame", "mp"), None),
        P(),
        P("dp", None, ("frame", "mp")),
    )
    return jax.shard_map(
        shards,
        mesh=mesh,
        in_specs=placed,
        out_specs=(P("dp", None, ("frame", "mp"), None), P()),
        check_vma=False,
    )
```

```python
import math

import jax
import jax.numpy as jnp
from jax import lax
from jax.experimental import pallas as pl
from jax.experimental.pallas import tpu as pltpu
from jax.sharding import PartitionSpec as P

F32 = jnp.float32
BF16 = jnp.bfloat16
MESH = pl.DeviceIdType.MESH

D = 768
HALF = D // 2
HD = 64
T_HEADS = 12
CODES = 1024
POS = 1024
FRAMES = 16
NX, NY, NZ = 4, 4, 8
SIZE = {"x": NX, "y": NY, "z": NZ}
ORDERS = (("x", "y", "z"), ("z", "y", "x"), ("z", "x", "y"))
UNITS = tuple(SIZE[order[0]] // 2 * 8 for order in ORDERS)
EVENTS = (
    (0, 0), (1, 0), (0, 1, 1), (2, 0), (0, 1, 3), (0, 1, 2),
    (0, 2, 1, 0), (1, 2, 1, 0), (1, 1, 1),
    (0, 2, 1, 1), (2, 1, 1), (1, 1, 3), (1, 1, 2), (0, 2, 1, 3),
    (0, 2, 1, 2), (2, 1, 3), (2, 1, 2), (2, 2, 1, 0),
    (0, 2, 2, 0), (0, 2, 2, 1), (0, 2, 2, 3), (1, 2, 2, 0),
    (0, 2, 2, 2), (2, 2, 1, 1), (0, 2, 3, 0), (1, 2, 1, 1),
    (0, 2, 3, 1), (2, 2, 1, 3), (0, 2, 3, 3), (1, 2, 1, 3),
    (0, 2, 3, 2), (2, 2, 1, 2), (1, 2, 1, 2),
    (2, 2, 2, 0), (0, 2, 4, 0), (0, 2, 4, 1), (1, 2, 2, 1), (2, 2, 2, 1),
    (0, 2, 4, 3), (1, 2, 2, 3), (0, 2, 4, 2), (2, 2, 2, 3), (1, 2, 2, 2), (2, 2, 2, 2),
)
GATHER_AT = (0, 0, 0, 1, 6, 21, 22, 26, 28, 29)
MLP_GROUPS = (
    (29, ((0, (0, 1, 7, 2)),)),
    (32, ((2, (0, 1)),)),
    (33, ((1, (0, 1)),)),
    (33, ((0, (6, 3, 5)), (1, (3,)))),
    (41, ((2, (3,)), (0, (4,)))),
    (44, ((1, (2,)), (2, (2,)))),
)
SOURCES = {"x": ((0, 1), (2, 3)), "z": ((0, 1), (2, 7), (6, 3), (4, 5))}


def layer_norm(values, gain):
    center = jnp.mean(values, axis=-1, keepdims=True)
    shifted = values - center
    spread = jnp.mean(shifted * shifted, axis=-1, keepdims=True)
    return shifted * lax.rsqrt(spread + 1e-06) * gain


def nt_dot(a, b):
    return lax.dot_general(a, b, (((1,), (1,)), ((), ())), preferred_element_type=F32)


def gelu(v):
    inner = math.sqrt(2.0 / math.pi) * (v + 0.044715 * (v * v * v))
    return 0.5 * v * (1.0 + jnp.tanh(inner))


def lanes(shape):
    return lax.broadcasted_iota(jnp.int32, shape, len(shape) - 1)


def block_kernel(
    frames_hbm, gs_hbm, sproj_hbm, sout_hbm, gt_hbm, tproj_hbm, tout_hbm, gm_hbm,
    win_hbm, wout_hbm, cproj_hbm, cidx_hbm,
    out_hbm, means_ref,
    fr, gs_ref, sp, so, gt_ref, tp, to, gm_ref, win_ref, wout_ref, cproj_ref, cidx_ref,
    q_s, k_s, v_s,
    heads_send, heads_recv, rows_send, rows_recv,
    own_parts, first0, first1, first2, w0, w1, w2,
    cidx_recv, hot, count_send, count_recv, count_all,
    act_send, act_recv, back_send, back_recv,
    out_s, red_send, red_recv, tot_all, mean_send, mean_recv,
    load_sem, heads_ss, heads_rs, rows_ss, rows_rs, first_ss, first_rs,
    second_ss, second_rs,    ring_ss, ring_rs, pair_ss, pair_rs, red_ss, red_rs, tot_ss, tot_rs, fin_ss, fin_rs,
    count_ss, count_rs, all_count_ss, all_count_rs,
):
    c = lax.axis_index("dp")
    f = lax.axis_index("frame")
    m = lax.axis_index("mp")
    me = {"x": f // NY, "y": f % NY, "z": m}
    group = c * NZ + m

    def at(**moved):
        x = moved.get("x", me["x"])
        y = moved.get("y", me["y"])
        return (c, x * NY + y, moved.get("z", m))

    def frame_peer(k):
        return (c, (f + k) % FRAMES, m)

    def group_peer(k):
        other = (group + k) % 16
        return (other // NZ, f, other % NZ)

    barrier = pltpu.get_barrier_semaphore()

    @pl.loop(1, 16)
    def _(k):
        pl.semaphore_signal(barrier, inc=1, device_id=frame_peer(k), device_id_type=MESH)
        pl.semaphore_signal(barrier, inc=1, device_id=group_peer(k), device_id_type=MESH)

    loads = {}
    for name, src, dst in (
        ("win", win_hbm, win_ref), ("wout", wout_hbm, wout_ref),
        ("gs", gs_hbm, gs_ref), ("sp", sproj_hbm, sp), ("fr", frames_hbm.at[0, 0], fr),
        ("so", sout_hbm, so), ("gt", gt_hbm, gt_ref), ("tp", tproj_hbm, tp),
        ("to", tout_hbm, to), ("gm", gm_hbm, gm_ref),
        ("cproj", cproj_hbm, cproj_ref), ("cidx", cidx_hbm, cidx_ref),
    ):
        loads[name] = pltpu.make_async_copy(src, dst, load_sem.at[len(loads)])
        loads[name].start()
    loads["win"].wait()
    loads["wout"].wait()

    win = win_ref[...].astype(F32)
    wout = wout_ref[...].astype(F32)
    for p in range(3):
        own_parts[p] = jnp.concatenate(
            [win[p * 8 : p * 8 + 8], wout[p * 8 : p * 8 + 8]], axis=0
        ).astype(BF16)
    firsts = (first0, first1, first2)
    gathered = (w0, w1, w2)

    def first_copy(p, slot):
        axis = ORDERS[p][0]
        zero, one = SOURCES[axis][slot]
        back = SIZE[axis] - zero - c * (one - zero)
        return pltpu.make_async_remote_copy(
            src_ref=own_parts.at[p], dst_ref=firsts[p].at[slot],
            send_sem=first_ss.at[p, slot], recv_sem=first_rs.at[p, slot],
            device_id=at(**{axis: (me[axis] + back) % SIZE[axis]}), device_id_type=MESH,
        )

    def first_send(p):
        for slot in range(1, len(SOURCES[ORDERS[p][0]])):
            first_copy(p, slot).start()

        @pl.when(c == 1)
        def _():
            first_copy(p, 0).start()

        @pl.when(c == 0)
        def _():
            firsts[p][0] = own_parts[p]

    def first_wait(p):
        n = SIZE[ORDERS[p][0]]
        for slot in range(1, n // 2):
            first_copy(p, slot).wait_recv()

        @pl.when(c == 1)
        def _():
            first_copy(p, 0).wait_recv()

        block = firsts[p][...].astype(F32).reshape(n // 2, 2, 8, D)
        at3, at2 = me[ORDERS[p][2]], me[ORDERS[p][1]]
        for side in range(2):
            gathered[p][at3, at2, side] = block[:, side].reshape(n // 2 * 8, D).astype(BF16)

    def first_done(p):
        for slot in range(1, len(SOURCES[ORDERS[p][0]])):
            first_copy(p, slot).wait_send()

        @pl.when(c == 1)
        def _():
            first_copy(p, 0).wait_send()

    def second_copy(p, k):
        _, axis, last = ORDERS[p]
        block = gathered[p].at[me[last], me[axis]]
        return pltpu.make_async_remote_copy(
            src_ref=block, dst_ref=block,
            send_sem=second_ss.at[p, k], recv_sem=second_rs.at[p, k],
            device_id=at(**{axis: (me[axis] + k) % SIZE[axis]}), device_id_type=MESH,
        )

    def ring_copy(p, step, sub, way):
        _, inner, axis = ORDERS[p]
        n = SIZE[axis]
        shift = (n - (step - 1)) if way == 0 else (step - 1)
        block = gathered[p].at[
            (me[axis] + shift) % n, (me[inner] + SIZE[inner] - sub) % SIZE[inner]
        ]
        if step == n // 2:
            block = block.at[way]
        return pltpu.make_async_remote_copy(
            src_ref=block, dst_ref=block,
            send_sem=ring_ss.at[p, step - 1, sub, way],
            recv_sem=ring_rs.at[p, step - 1, sub, way],
            device_id=at(**{axis: (me[axis] + (1 if way == 0 else n - 1)) % n}),
            device_id_type=MESH,
        )

    def ring_send(p, step, sub):
        if step <= SIZE[ORDERS[p][2]] // 2:
            for way in range(2):
                ring_copy(p, step, sub, way).start()

    todo = list(EVENTS)

    def gather(until):
        count = until - len(EVENTS) + len(todo)
        for event in todo[:count]:
            p = event[0]
            if event[1] == 0:
                first_wait(p)
                for k in (1, 3, 2):
                    second_copy(p, k).start()
                ring_send(p, 1, 0)
            elif event[1] == 1:
                second_copy(p, event[2]).wait_recv()
                ring_send(p, 1, event[2])
            else:
                for way in range(2):
                    ring_copy(p, event[2], event[3], way).wait_recv()
                ring_send(p, event[2] + 1, event[3])
        del todo[:count]

    def gather_sent():
        for p in range(3):
            first_done(p)
            for k in range(1, 4):
                second_copy(p, k).wait_send()
            for step in range(1, SIZE[ORDERS[p][2]] // 2 + 1):
                for sub in range(4):
                    for way in range(2):
                        ring_copy(p, step, sub, way).wait_send()

    for name in ("gs", "sp", "fr"):
        loads[name].wait()
    wqkv = jnp.concatenate([sp[...].reshape(3 * HD, D), jnp.zeros((HD, D), BF16)], axis=0)
    gain_space = gs_ref[...].reshape(1, D)

    @pl.loop(0, 4)
    def _(i):
        rows = pl.ds(pl.multiple_of(i * 256, 256), 256)
        normed = layer_norm(fr[rows, :].astype(F32), gain_space).astype(BF16)
        both = nt_dot(normed, wqkv)
        qk = both[:, :128]
        low = lanes((256, 128)) < HD
        k_s[rows, :] = pltpu.roll(qk, HD, 1).astype(BF16)
        v = both[:, 128:]
        v_s[rows, :] = jnp.where(low, v, 1.0).astype(BF16)
        q = jnp.where(low, qk * (1.0 / math.sqrt(HD)), 0.0).reshape(4, NZ, 8, 128)
        for to_m in range(NZ):
            q_s[to_m, pl.ds(pl.multiple_of(i * 32, 32), 32), :] = (
                q[:, to_m].reshape(32, 128).astype(BF16)
            )

    partner = (1 - c, f, m)

    def pair_copy(i, src, dst):
        return pltpu.make_async_remote_copy(
            src_ref=src, dst_ref=dst, send_sem=pair_ss.at[i], recv_sem=pair_rs.at[i],
            device_id=partner, device_id_type=MESH,
        )

    for name in ("gt", "tp", "to", "gm", "cproj", "cidx"):
        loads[name].wait()
    pl.semaphore_wait(barrier, 30)
    for p in range(3):
        first_send(p)
    codes_copy = pair_copy(2, cidx_ref, cidx_recv)
    codes_copy.start()

    def heads_copy(shift):
        dest = (m + shift) % NZ
        return pltpu.make_async_remote_copy(
            src_ref=heads_send.at[dest], dst_ref=heads_recv.at[m],
            send_sem=heads_ss.at[shift], recv_sem=heads_rs.at[shift],
            device_id=(c, f, dest), device_id_type=MESH,
        )

    half = lanes((64, 128)) < HD
    for i, shifts in enumerate(((4, 3), (5, 2), (6, 1), (7, 0))):
        queries = jnp.concatenate([q_s[(m + shift) % NZ] for shift in shifts], axis=0)
        scores = nt_dot(queries, k_s[...])
        weights = jnp.exp(scores - jnp.max(scores, axis=-1, keepdims=True)).astype(BF16)
        mixed = jnp.dot(weights, v_s[...], preferred_element_type=F32)
        turned = pltpu.roll(mixed, HD, 1)
        for j, shift in enumerate(shifts):
            top, bottom = slice(j * 128, j * 128 + 64), slice(j * 128 + 64, j * 128 + 128)
            heads_send[(m + shift) % NZ] = (
                jnp.where(half, mixed[top], turned[bottom])
                / jnp.where(half, turned[top], mixed[bottom])
            ).astype(BF16)
        for shift in shifts:
            if shift:
                heads_copy(shift).start()
        gather(GATHER_AT[i])

    heads_recv[m] = heads_send[m]

    def onehot(codes):
        codes = jnp.broadcast_to(codes, (FRAMES, 8, FRAMES)).reshape(128, FRAMES)
        diagonal = lax.broadcasted_iota(jnp.int32, (128, FRAMES), 0) // 8 == lanes((128, FRAMES))
        codes = jnp.sum(jnp.where(diagonal, codes, 0), axis=1, keepdims=True)
        return (codes == lanes((128, CODES))).astype(F32).astype(BF16)

    def count_copy(k):
        dest = (m + k) % NZ
        return pltpu.make_async_remote_copy(
            src_ref=count_send.at[dest], dst_ref=count_recv.at[k], send_sem=count_ss.at[k],
            recv_sem=count_rs.at[k], device_id=(c, f, dest), device_id_type=MESH,
        )

    def all_count_copy(k):
        return pltpu.make_async_remote_copy(
            src_ref=count_all.at[f], dst_ref=count_all.at[f], send_sem=all_count_ss.at[k],
            recv_sem=all_count_rs.at[k], device_id=frame_peer(k), device_id_type=MESH,
        )

    codes_copy.wait_recv()
    hot[:128] = onehot(cidx_recv[...])
    hot[128:] = onehot(cidx_ref[...])
    counts = jnp.dot(jnp.ones((16, 256), BF16), hot[...], preferred_element_type=F32)
    for dest in range(NZ):
        count_send[dest] = counts[:, dest * 128 : dest * 128 + 128].astype(BF16)
    for k in range(1, NZ):
        count_copy(k).start()
    count_recv[0] = count_send[m]
    gather(GATHER_AT[4])
    for k in range(1, NZ):
        heads_copy(k).wait_recv()

    side = lanes((64, 128)) < HD
    upper, lower = [], []
    for i in range(NZ // 2):
        even = heads_recv[2 * i].astype(F32)
        odd = heads_recv[2 * i + 1].astype(F32)
        upper.append(jnp.where(side, even, pltpu.roll(odd, HD, 1)))
        lower.append(jnp.where(side, pltpu.roll(even, HD, 1), odd))
    heads_all = jnp.concatenate(
        [jnp.concatenate(upper, axis=1), jnp.concatenate(lower, axis=1)], axis=0
    ).astype(BF16)
    own = []
    for i in range(FRAMES):
        pair = fr[pl.ds(pl.multiple_of(i * 64 + (m // 2) * 16, 16), 16), :].astype(F32)
        own.append(jnp.where(m % 2 == 0, pair[:8], pair[8:]))
    loads["so"].wait()
    after_space = jnp.concatenate(own, axis=0) + jnp.dot(
        heads_all, so[...], preferred_element_type=F32
    )
    split = after_space.reshape(FRAMES, 8, D)
    rows_send[...] = jnp.concatenate([split[:, :, :HALF], split[:, :, HALF:]], axis=1).astype(BF16)

    def rows_copy(k):
        dest = (f + k) % FRAMES
        return pltpu.make_async_remote_copy(
            src_ref=rows_send.at[dest], dst_ref=rows_recv.at[f],
            send_sem=rows_ss.at[k], recv_sem=rows_rs.at[k],
            device_id=(c, dest, m), device_id_type=MESH,
        )

    @pl.loop(1, FRAMES)
    def _(k):
        rows_copy(k).start()

    rows_recv[f] = rows_send[f]
    for k in range(1, NZ):
        count_copy(k).wait_recv()
    counts = jnp.sum(count_recv[...].astype(F32), axis=0)
    upper = jnp.floor(counts[:8] * (1.0 / 256.0))
    count_all[f] = jnp.concatenate([counts[8:] - 256.0 * upper, upper], axis=0).astype(BF16)

    @pl.loop(1, FRAMES)
    def _(k):
        all_count_copy(k).start()

    gather(GATHER_AT[5])

    @pl.loop(1, FRAMES)
    def _(k):
        rows_copy(k).wait_recv()

    arrived = rows_recv[...].astype(F32)
    after_space = jnp.concatenate([arrived[:, :8], arrived[:, 8:]], axis=2).reshape(128, D)
    time_in = layer_norm(after_space, gt_ref[...].reshape(1, D)).astype(BF16)
    tq = jnp.dot(time_in, tp[0], preferred_element_type=F32) * (1.0 / math.sqrt(HD))
    tk = jnp.dot(time_in, tp[1], preferred_element_type=F32).astype(BF16)
    tv = jnp.dot(time_in, tp[2], preferred_element_type=F32).astype(BF16)
    tq = tq.astype(BF16)
    gather(GATHER_AT[6])
    row = lax.broadcasted_iota(jnp.int32, (128, 128), 0)
    col = lax.broadcasted_iota(jnp.int32, (128, 128), 1)
    seen = ((row % 8 == col % 8) & (col // 8 <= row // 8))[None]
    low = col < HD
    none = jnp.zeros((128, 128), BF16)
    ones = jnp.ones((128, 128), BF16)
    cuts = [slice(i * 128, i * 128 + 128) for i in range(T_HEADS // 2)]
    scores = jnp.concatenate(
        [
            nt_dot(
                jnp.concatenate(
                    [jnp.where(low, tq[:, cut], none), jnp.where(low, none, tq[:, cut])], axis=0
                ),
                tk[:, cut],
            )
            for cut in cuts
        ],
        axis=0,
    ).reshape(T_HEADS, 128, 128)
    scores = jnp.where(seen, scores, -jnp.inf)
    weights = jnp.exp(scores - jnp.max(scores, axis=-1, keepdims=True)).astype(BF16)
    gather(GATHER_AT[7])
    pieces = []
    for i, cut in enumerate(cuts):
        both = jnp.dot(
            weights[2 * i : 2 * i + 2].reshape(256, 128),
            jnp.concatenate([tv[:, cut], ones], axis=1),
            preferred_element_type=F32,
        )
        both = both[:, :128] / both[:, 128:]
        pieces.append(jnp.where(low, both[:128], both[128:]).astype(BF16))
    gather(GATHER_AT[8])
    time_heads = jnp.concatenate(pieces, axis=1)
    after_time = after_space + jnp.dot(time_heads, to[...], preferred_element_type=F32)
    gather(GATHER_AT[9])
    act_send[...] = layer_norm(after_time, gm_ref[...].reshape(1, D)).astype(BF16)

    act_copy = pair_copy(0, act_send, act_recv)
    act_copy.start()
    act_copy.wait_recv()
    act = jnp.concatenate([act_recv[...], act_send[...]], axis=0)
    partial = jnp.zeros((256, D), F32)
    for until, group_of in MLP_GROUPS:
        gather(until)
        w_in, w_out = [], []
        for p, steps in group_of:
            for step in steps:
                block = gathered[p][(me[ORDERS[p][2]] + step) % SIZE[ORDERS[p][2]]]
                w_in.append(block[:, 0].reshape(-1, D))
                w_out.append(block[:, 1].reshape(-1, D))
        hidden = gelu(nt_dot(act, jnp.concatenate(w_in, axis=0))).astype(BF16)
        partial += jnp.dot(hidden, jnp.concatenate(w_out, axis=0), preferred_element_type=F32)

    def red_copy(k):
        return pltpu.make_async_remote_copy(
            src_ref=red_send.at[(group + k) % 16], dst_ref=red_recv.at[k], send_sem=red_ss.at[k],
            recv_sem=red_rs.at[k], device_id=group_peer(k), device_id_type=MESH,
        )

    after_time = after_time + partial[128:]
    share = jnp.concatenate([partial[:128], after_time], axis=0).astype(BF16)
    vecs = nt_dot(cproj_ref[...], share)
    high = vecs.astype(BF16)
    rest = (vecs - high.astype(F32)).astype(BF16)
    sums = jnp.dot(
        jnp.concatenate([high, rest], axis=0), hot[...], preferred_element_type=F32
    )
    sums = sums[:32] + sums[32:]
    for dest in range(16):
        low_row, low_lane = dest // NZ * 16, dest % NZ * 128
        red_send[dest] = sums[low_row : low_row + 16, low_lane : low_lane + 128].astype(BF16)

    @pl.loop(1, 16)
    def _(k):
        red_copy(k).start()

    back_send[...] = partial[:128]
    back_copy = pair_copy(1, back_send, back_recv)
    back_copy.start()

    def tot_copy(k):
        return pltpu.make_async_remote_copy(
            src_ref=tot_all.at[f], dst_ref=tot_all.at[f], send_sem=tot_ss.at[k],
            recv_sem=tot_rs.at[k], device_id=frame_peer(k), device_id_type=MESH,
        )

    def mean_copy(k):
        return pltpu.make_async_remote_copy(
            src_ref=mean_send, dst_ref=mean_recv.at[group], send_sem=fin_ss.at[k],
            recv_sem=fin_rs.at[k], device_id=group_peer(k), device_id_type=MESH,
        )

    gather_sent()
    red_recv[0] = red_send[group]

    @pl.loop(1, 16)
    def _(k):
        red_copy(k).wait_recv()

    tot_all[f] = jnp.sum(red_recv[...].astype(F32), axis=0).astype(BF16)

    @pl.loop(1, 16)
    def _(k):
        tot_copy(k).start()

    back_copy.wait_recv()
    outputs = (after_time + back_recv[...]).reshape(FRAMES, 8, D)
    out_s[0] = outputs.astype(BF16)
    out_copy = pltpu.make_async_copy(out_s, out_hbm, load_sem.at[0])
    out_copy.start()
    for k in range(1, NZ):
        heads_copy(k).wait_send()
        count_copy(k).wait_send()
    for copy in (codes_copy, act_copy, back_copy):
        copy.wait_send()

    @pl.loop(1, 16)
    def _(k):
        rows_copy(k).wait_send()
        red_copy(k).wait_send()
        all_count_copy(k).wait_send()
        all_count_copy(k).wait_recv()

    counts = jnp.sum(count_all[...].astype(F32), axis=0)
    counts = jnp.maximum(counts[:8] + 256.0 * counts[8:], 1.0)
    counts = jnp.concatenate([counts, counts], axis=0)

    @pl.loop(1, 16)
    def _(k):
        tot_copy(k).wait_recv()

    means = (jnp.sum(tot_all[...].astype(F32), axis=0) / counts).astype(BF16)
    mean_send[...] = means
    mean_recv[group] = means

    @pl.loop(1, 16)
    def _(k):
        mean_copy(k).start()

    @pl.loop(1, 16)
    def _(k):
        tot_copy(k).wait_send()
        mean_copy(k).wait_send()

    out_copy.wait()

    @pl.loop(1, 16)
    def _(k):
        mean_copy(k).wait_recv()

    for g in range(16):
        cut = slice(g % NZ * 128, g % NZ * 128 + 128)
        means_ref[g // NZ * 16 : g // NZ * 16 + 16, cut] = mean_recv[g].astype(F32)


def shards(*args):
    args = list(args)
    args[2] = args[2].swapaxes(1, 2)
    args[10] = args[10].T
    args[11] = args[11].swapaxes(1, 2)
    args = [pltpu.with_memory_space_constraint(arg, pltpu.HBM) for arg in args]
    vmem = pl.BlockSpec(memory_space=pltpu.VMEM)
    hbm = pl.BlockSpec(memory_space=pltpu.HBM)
    dma = pltpu.SemaphoreType.DMA
    scratch = [
        pltpu.VMEM((POS, D), BF16),
        pltpu.VMEM((D,), F32),
        pltpu.VMEM((3, HD, D), BF16),
        pltpu.VMEM((512, D), BF16),
        pltpu.VMEM((D,), F32),
        pltpu.VMEM((3, D, D), BF16),
        pltpu.VMEM((D, D), BF16),
        pltpu.VMEM((D,), F32),
        pltpu.VMEM((24, D), BF16),
        pltpu.VMEM((24, D), BF16),
        pltpu.VMEM((32, D), BF16),
        pltpu.VMEM((1, 8, FRAMES), jnp.int32),
        pltpu.VMEM((NZ, 128, 128), BF16),
        pltpu.VMEM((POS, 128), BF16),
        pltpu.VMEM((POS, 128), BF16),
        pltpu.VMEM((NZ, 64, 128), BF16),
        pltpu.VMEM((NZ, 64, 128), BF16),
        pltpu.VMEM((FRAMES, 16, HALF), BF16),
        pltpu.VMEM((FRAMES, 16, HALF), BF16),
        pltpu.VMEM((3, 16, D), BF16),
    ]
    scratch += [pltpu.VMEM((SIZE[order[0]] // 2, 16, D), BF16) for order in ORDERS]
    scratch += [
        pltpu.VMEM((SIZE[order[2]], SIZE[order[1]], 2, units, D), BF16)
        for order, units in zip(ORDERS, UNITS)
    ]
    scratch += [
        pltpu.VMEM((1, 8, FRAMES), jnp.int32),
        pltpu.VMEM((256, CODES), BF16),
        pltpu.VMEM((NZ, 16, 128), BF16),
        pltpu.VMEM((NZ, 16, 128), BF16),
        pltpu.VMEM((FRAMES, 16, 128), BF16),
        pltpu.VMEM((128, D), BF16),
        pltpu.VMEM((128, D), BF16),
        pltpu.VMEM((128, D), F32),
        pltpu.VMEM((128, D), F32),
        pltpu.VMEM((1, FRAMES, 8, D), BF16),
        pltpu.VMEM((16, 16, 128), BF16),
        pltpu.VMEM((16, 16, 128), BF16),
        pltpu.VMEM((FRAMES, 16, 128), BF16),
        pltpu.VMEM((16, 128), BF16),
        pltpu.VMEM((16, 16, 128), BF16),
    ]
    scratch += [
        dma((12,)),
        dma((NZ,)), dma((NZ,)),
        dma((FRAMES,)), dma((FRAMES,)),
        dma((3, NZ)), dma((3, NZ)),
        dma((3, 4)), dma((3, 4)),
        dma((3, 4, 4, 2)), dma((3, 4, 4, 2)),
        dma((3,)), dma((3,)),
        dma((16,)), dma((16,)),
        dma((16,)), dma((16,)),
        dma((16,)), dma((16,)),
        dma((NZ,)), dma((NZ,)),
        dma((16,)), dma((16,)),
    ]
    block_out, means = pl.pallas_call(
        block_kernel,
        out_shape=(
            jax.ShapeDtypeStruct((1, FRAMES, 8, D), BF16),
            jax.ShapeDtypeStruct((32, CODES), F32),
        ),
        in_specs=[hbm] * 12,
        out_specs=(hbm, vmem),
        scratch_shapes=scratch,
        compiler_params=pltpu.CompilerParams(
            collective_id=0, has_side_effects=True, vmem_limit_bytes=52 * 1024 * 1024
        ),
    )(*args)
    return block_out, means.T


def solution(mesh):
    placed = (
        P("dp", "frame", None, None),
        P(),
        P(None, None, "mp"),
        P(),
        P(),
        P(),
        P(),
        P(),
        P(("frame", "mp"), None),
        P(("frame", "mp"), None),
        P(),
        P("dp", None, ("frame", "mp")),
    )
    return jax.shard_map(
        shards,
        mesh=mesh,
        in_specs=placed,
        out_specs=(P("dp", None, ("frame", "mp"), None), P()),
        check_vma=False,
    )
```

```python
import math

import jax
import jax.numpy as jnp
from jax import lax
from jax.experimental import pallas as pl
from jax.experimental.pallas import tpu as pltpu
from jax.sharding import PartitionSpec as P

F32 = jnp.float32
BF16 = jnp.bfloat16
MESH = pl.DeviceIdType.MESH

D = 768
HALF = D // 2
HD = 64
T_HEADS = 12
CODES = 1024
POS = 1024
FRAMES = 16
NX, NY, NZ = 4, 4, 8
SIZE = {"x": NX, "y": NY, "z": NZ}
ORDERS = (("x", "y", "z"), ("z", "y", "x"), ("z", "x", "y"))
UNITS = tuple(SIZE[order[0]] // 2 * 8 for order in ORDERS)
EVENTS = (
    (0, 0), (1, 0), (0, 1, 1), (2, 0), (0, 1, 3), (0, 1, 2),
    (0, 2, 1, 0), (1, 2, 1, 0), (1, 1, 1),
    (0, 2, 1, 1), (2, 1, 1), (1, 1, 3), (1, 1, 2), (0, 2, 1, 3),
    (0, 2, 1, 2), (2, 1, 3), (2, 1, 2), (2, 2, 1, 0),
    (0, 2, 2, 0), (0, 2, 2, 1), (0, 2, 2, 3), (1, 2, 2, 0),
    (0, 2, 2, 2), (2, 2, 1, 1), (0, 2, 3, 0), (1, 2, 1, 1),
    (0, 2, 3, 1), (2, 2, 1, 3), (0, 2, 3, 3), (1, 2, 1, 3),
    (0, 2, 3, 2), (2, 2, 1, 2), (1, 2, 1, 2),
    (2, 2, 2, 0), (0, 2, 4, 0), (0, 2, 4, 1), (1, 2, 2, 1), (2, 2, 2, 1),
    (0, 2, 4, 3), (1, 2, 2, 3), (0, 2, 4, 2), (2, 2, 2, 3), (1, 2, 2, 2), (2, 2, 2, 2),
)
GATHER_AT = (0, 1, 1, 1, 6, 23, 24, 27, 28, 29)
MLP_GROUPS = (
    (29, ((0, (0, 1, 7, 2)),)),
    (32, ((2, (0, 1)),)),
    (33, ((1, (0, 1)),)),
    (33, ((0, (6, 3, 5)), (1, (3,)))),
    (41, ((2, (3,)), (0, (4,)))),
    (44, ((1, (2,)), (2, (2,)))),
)
SOURCES = {"x": ((0, 1), (2, 3)), "z": ((0, 1), (2, 7), (6, 3), (4, 5))}


def layer_norm(values, gain):
    center = jnp.mean(values, axis=-1, keepdims=True)
    shifted = values - center
    spread = jnp.mean(shifted * shifted, axis=-1, keepdims=True)
    return shifted * lax.rsqrt(spread + 1e-06) * gain


def nt_dot(a, b):
    return lax.dot_general(a, b, (((1,), (1,)), ((), ())), preferred_element_type=F32)


def gelu(v):
    inner = math.sqrt(2.0 / math.pi) * (v + 0.044715 * (v * v * v))
    return 0.5 * v * (1.0 + jnp.tanh(inner))


def lanes(shape):
    return lax.broadcasted_iota(jnp.int32, shape, len(shape) - 1)


def block_kernel(
    frames_hbm, gs_hbm, sproj_hbm, sout_hbm, gt_hbm, tproj_hbm, tout_hbm, gm_hbm,
    win_hbm, wout_hbm, cproj_hbm, cidx_hbm,
    out_hbm, means_ref,
    fr, gs_ref, sp, so, gt_ref, tp, to, gm_ref, win_ref, wout_ref, cproj_ref, cidx_ref,
    q_s, k_s, v_s,
    heads_send, heads_recv, rows_send, rows_recv,
    own_parts, first0, first1, first2, w0, w1, w2,
    cidx_recv, hot, count_send, count_recv, count_all,
    act_send, act_recv, back_send, back_recv,
    out_s, red_send, red_recv, tot_all, mean_send, mean_recv,
    load_sem, heads_ss, heads_rs, rows_ss, rows_rs, first_ss, first_rs,
    second_ss, second_rs,    ring_ss, ring_rs, pair_ss, pair_rs, red_ss, red_rs, tot_ss, tot_rs, fin_ss, fin_rs,
    count_ss, count_rs, all_count_ss, all_count_rs,
):
    c = lax.axis_index("dp")
    f = lax.axis_index("frame")
    m = lax.axis_index("mp")
    me = {"x": f // NY, "y": f % NY, "z": m}
    group = c * NZ + m

    def at(**moved):
        x = moved.get("x", me["x"])
        y = moved.get("y", me["y"])
        return (c, x * NY + y, moved.get("z", m))

    def frame_peer(k):
        return (c, (f + k) % FRAMES, m)

    def group_peer(k):
        other = (group + k) % 16
        return (other // NZ, f, other % NZ)

    barrier = pltpu.get_barrier_semaphore()

    @pl.loop(1, 16)
    def _(k):
        pl.semaphore_signal(barrier, inc=1, device_id=frame_peer(k), device_id_type=MESH)
        pl.semaphore_signal(barrier, inc=1, device_id=group_peer(k), device_id_type=MESH)

    loads = {}
    for name, src, dst in (
        ("win", win_hbm, win_ref), ("wout", wout_hbm, wout_ref),
        ("gs", gs_hbm, gs_ref), ("sp", sproj_hbm, sp), ("fr", frames_hbm.at[0, 0], fr),
        ("so", sout_hbm, so), ("gt", gt_hbm, gt_ref), ("tp", tproj_hbm, tp),
        ("to", tout_hbm, to), ("gm", gm_hbm, gm_ref),
        ("cproj", cproj_hbm, cproj_ref), ("cidx", cidx_hbm, cidx_ref),
    ):
        loads[name] = pltpu.make_async_copy(src, dst, load_sem.at[len(loads)])
        loads[name].start()
    loads["win"].wait()
    loads["wout"].wait()

    win = win_ref[...].astype(F32)
    wout = wout_ref[...].astype(F32)
    for p in range(3):
        own_parts[p] = jnp.concatenate(
            [win[p * 8 : p * 8 + 8], wout[p * 8 : p * 8 + 8]], axis=0
        ).astype(BF16)
    firsts = (first0, first1, first2)
    gathered = (w0, w1, w2)

    def first_copy(p, slot):
        axis = ORDERS[p][0]
        zero, one = SOURCES[axis][slot]
        back = SIZE[axis] - zero - c * (one - zero)
        return pltpu.make_async_remote_copy(
            src_ref=own_parts.at[p], dst_ref=firsts[p].at[slot],
            send_sem=first_ss.at[p, slot], recv_sem=first_rs.at[p, slot],
            device_id=at(**{axis: (me[axis] + back) % SIZE[axis]}), device_id_type=MESH,
        )

    def first_send(p):
        for slot in range(1, len(SOURCES[ORDERS[p][0]])):
            first_copy(p, slot).start()

        @pl.when(c == 1)
        def _():
            first_copy(p, 0).start()

        @pl.when(c == 0)
        def _():
            firsts[p][0] = own_parts[p]

    def first_wait(p):
        n = SIZE[ORDERS[p][0]]
        for slot in range(1, n // 2):
            first_copy(p, slot).wait_recv()

        @pl.when(c == 1)
        def _():
            first_copy(p, 0).wait_recv()

        block = firsts[p][...].astype(F32).reshape(n // 2, 2, 8, D)
        at3, at2 = me[ORDERS[p][2]], me[ORDERS[p][1]]
        for side in range(2):
            gathered[p][at3, at2, side] = block[:, side].reshape(n // 2 * 8, D).astype(BF16)

    def first_done(p):
        for slot in range(1, len(SOURCES[ORDERS[p][0]])):
            first_copy(p, slot).wait_send()

        @pl.when(c == 1)
        def _():
            first_copy(p, 0).wait_send()

    def second_copy(p, k):
        _, axis, last = ORDERS[p]
        block = gathered[p].at[me[last], me[axis]]
        return pltpu.make_async_remote_copy(
            src_ref=block, dst_ref=block,
            send_sem=second_ss.at[p, k], recv_sem=second_rs.at[p, k],
            device_id=at(**{axis: (me[axis] + k) % SIZE[axis]}), device_id_type=MESH,
        )

    def ring_copy(p, step, sub, way):
        _, inner, axis = ORDERS[p]
        n = SIZE[axis]
        shift = (n - (step - 1)) if way == 0 else (step - 1)
        block = gathered[p].at[
            (me[axis] + shift) % n, (me[inner] + SIZE[inner] - sub) % SIZE[inner]
        ]
        if step == n // 2:
            block = block.at[way]
        return pltpu.make_async_remote_copy(
            src_ref=block, dst_ref=block,
            send_sem=ring_ss.at[p, step - 1, sub, way],
            recv_sem=ring_rs.at[p, step - 1, sub, way],
            device_id=at(**{axis: (me[axis] + (1 if way == 0 else n - 1)) % n}),
            device_id_type=MESH,
        )

    def ring_send(p, step, sub):
        if step <= SIZE[ORDERS[p][2]] // 2:
            for way in range(2):
                ring_copy(p, step, sub, way).start()

    todo = list(EVENTS)

    def gather(until):
        count = until - len(EVENTS) + len(todo)
        for event in todo[:count]:
            p = event[0]
            if event[1] == 0:
                first_wait(p)
                for k in (1, 3, 2):
                    second_copy(p, k).start()
                ring_send(p, 1, 0)
            elif event[1] == 1:
                second_copy(p, event[2]).wait_recv()
                ring_send(p, 1, event[2])
            else:
                for way in range(2):
                    ring_copy(p, event[2], event[3], way).wait_recv()
                ring_send(p, event[2] + 1, event[3])
        del todo[:count]

    def gather_sent():
        for p in range(3):
            first_done(p)
            for k in range(1, 4):
                second_copy(p, k).wait_send()
            for step in range(1, SIZE[ORDERS[p][2]] // 2 + 1):
                for sub in range(4):
                    for way in range(2):
                        ring_copy(p, step, sub, way).wait_send()

    partner = (1 - c, f, m)

    def pair_copy(i, src, dst):
        return pltpu.make_async_remote_copy(
            src_ref=src, dst_ref=dst, send_sem=pair_ss.at[i], recv_sem=pair_rs.at[i],
            device_id=partner, device_id_type=MESH,
        )

    loads["cidx"].wait()
    pl.semaphore_wait(barrier, 30)
    for p in range(3):
        first_send(p)
    codes_copy = pair_copy(2, cidx_ref, cidx_recv)
    codes_copy.start()

    for name in ("gs", "sp", "fr"):
        loads[name].wait()
    wqkv = jnp.concatenate([sp[...].reshape(3 * HD, D), jnp.zeros((HD, D), BF16)], axis=0)
    gain_space = gs_ref[...].reshape(1, D)

    @pl.loop(0, 4)
    def _(i):
        rows = pl.ds(pl.multiple_of(i * 256, 256), 256)
        normed = layer_norm(fr[rows, :].astype(F32), gain_space).astype(BF16)
        both = nt_dot(normed, wqkv)
        qk = both[:, :128]
        low = lanes((256, 128)) < HD
        k_s[rows, :] = pltpu.roll(qk, HD, 1).astype(BF16)
        v = both[:, 128:]
        v_s[rows, :] = jnp.where(low, v, 1.0).astype(BF16)
        q = jnp.where(low, qk * (1.0 / math.sqrt(HD)), 0.0).reshape(4, NZ, 8, 128)
        for to_m in range(NZ):
            q_s[to_m, pl.ds(pl.multiple_of(i * 32, 32), 32), :] = (
                q[:, to_m].reshape(32, 128).astype(BF16)
            )

    def heads_copy(shift):
        dest = (m + shift) % NZ
        return pltpu.make_async_remote_copy(
            src_ref=heads_send.at[dest], dst_ref=heads_recv.at[m],
            send_sem=heads_ss.at[shift], recv_sem=heads_rs.at[shift],
            device_id=(c, f, dest), device_id_type=MESH,
        )

    half = lanes((64, 128)) < HD
    for i, shifts in enumerate(((4, 3), (5, 2), (6, 1), (7, 0))):
        queries = jnp.concatenate([q_s[(m + shift) % NZ] for shift in shifts], axis=0)
        scores = nt_dot(queries, k_s[...])
        weights = jnp.exp(scores - jnp.max(scores, axis=-1, keepdims=True)).astype(BF16)
        mixed = jnp.dot(weights, v_s[...], preferred_element_type=F32)
        turned = pltpu.roll(mixed, HD, 1)
        for j, shift in enumerate(shifts):
            top, bottom = slice(j * 128, j * 128 + 64), slice(j * 128 + 64, j * 128 + 128)
            heads_send[(m + shift) % NZ] = (
                jnp.where(half, mixed[top], turned[bottom])
                / jnp.where(half, turned[top], mixed[bottom])
            ).astype(BF16)
        for shift in shifts:
            if shift:
                heads_copy(shift).start()
        gather(GATHER_AT[i])

    heads_recv[m] = heads_send[m]

    def onehot(codes):
        codes = jnp.broadcast_to(codes, (FRAMES, 8, FRAMES)).reshape(128, FRAMES)
        diagonal = lax.broadcasted_iota(jnp.int32, (128, FRAMES), 0) // 8 == lanes((128, FRAMES))
        codes = jnp.sum(jnp.where(diagonal, codes, 0), axis=1, keepdims=True)
        return (codes == lanes((128, CODES))).astype(F32).astype(BF16)

    def count_copy(k):
        dest = (m + k) % NZ
        return pltpu.make_async_remote_copy(
            src_ref=count_send.at[dest], dst_ref=count_recv.at[k], send_sem=count_ss.at[k],
            recv_sem=count_rs.at[k], device_id=(c, f, dest), device_id_type=MESH,
        )

    def all_count_copy(k):
        return pltpu.make_async_remote_copy(
            src_ref=count_all.at[f], dst_ref=count_all.at[f], send_sem=all_count_ss.at[k],
            recv_sem=all_count_rs.at[k], device_id=frame_peer(k), device_id_type=MESH,
        )

    codes_copy.wait_recv()
    hot[:128] = onehot(cidx_recv[...])
    hot[128:] = onehot(cidx_ref[...])
    counts = jnp.dot(jnp.ones((16, 256), BF16), hot[...], preferred_element_type=F32)
    for dest in range(NZ):
        count_send[dest] = counts[:, dest * 128 : dest * 128 + 128].astype(BF16)
    for k in range(1, NZ):
        count_copy(k).start()
    count_recv[0] = count_send[m]
    gather(GATHER_AT[4])
    for k in range(1, NZ):
        heads_copy(k).wait_recv()

    side = lanes((64, 128)) < HD
    upper, lower = [], []
    for i in range(NZ // 2):
        even = heads_recv[2 * i].astype(F32)
        odd = heads_recv[2 * i + 1].astype(F32)
        upper.append(jnp.where(side, even, pltpu.roll(odd, HD, 1)))
        lower.append(jnp.where(side, pltpu.roll(even, HD, 1), odd))
    heads_all = jnp.concatenate(
        [jnp.concatenate(upper, axis=1), jnp.concatenate(lower, axis=1)], axis=0
    ).astype(BF16)
    own = []
    for i in range(FRAMES):
        pair = fr[pl.ds(pl.multiple_of(i * 64 + (m // 2) * 16, 16), 16), :].astype(F32)
        own.append(jnp.where(m % 2 == 0, pair[:8], pair[8:]))
    loads["so"].wait()
    after_space = jnp.concatenate(own, axis=0) + jnp.dot(
        heads_all, so[...], preferred_element_type=F32
    )
    split = after_space.reshape(FRAMES, 8, D)
    rows_send[...] = jnp.concatenate([split[:, :, :HALF], split[:, :, HALF:]], axis=1).astype(BF16)

    def rows_copy(k):
        dest = (f + k) % FRAMES
        return pltpu.make_async_remote_copy(
            src_ref=rows_send.at[dest], dst_ref=rows_recv.at[f],
            send_sem=rows_ss.at[k], recv_sem=rows_rs.at[k],
            device_id=(c, dest, m), device_id_type=MESH,
        )

    @pl.loop(1, FRAMES)
    def _(k):
        rows_copy(k).start()

    rows_recv[f] = rows_send[f]
    for k in range(1, NZ):
        count_copy(k).wait_recv()
    counts = jnp.sum(count_recv[...].astype(F32), axis=0)
    upper = jnp.floor(counts[:8] * (1.0 / 256.0))
    count_all[f] = jnp.concatenate([counts[8:] - 256.0 * upper, upper], axis=0).astype(BF16)

    @pl.loop(1, FRAMES)
    def _(k):
        all_count_copy(k).start()

    gather(GATHER_AT[5])

    @pl.loop(1, FRAMES)
    def _(k):
        rows_copy(k).wait_recv()

    for name in ("gt", "tp", "to", "gm", "cproj"):
        loads[name].wait()
    arrived = rows_recv[...].astype(F32)
    after_space = jnp.concatenate([arrived[:, :8], arrived[:, 8:]], axis=2).reshape(128, D)
    time_in = layer_norm(after_space, gt_ref[...].reshape(1, D)).astype(BF16)
    tq = jnp.dot(time_in, tp[0], preferred_element_type=F32) * (1.0 / math.sqrt(HD))
    tk = jnp.dot(time_in, tp[1], preferred_element_type=F32).astype(BF16)
    tv = jnp.dot(time_in, tp[2], preferred_element_type=F32).astype(BF16)
    tq = tq.astype(BF16)
    gather(GATHER_AT[6])
    row = lax.broadcasted_iota(jnp.int32, (128, 128), 0)
    col = lax.broadcasted_iota(jnp.int32, (128, 128), 1)
    seen = ((row % 8 == col % 8) & (col // 8 <= row // 8))[None]
    low = col < HD
    none = jnp.zeros((128, 128), BF16)
    ones = jnp.ones((128, 128), BF16)
    cuts = [slice(i * 128, i * 128 + 128) for i in range(T_HEADS // 2)]
    scores = jnp.concatenate(
        [
            nt_dot(
                jnp.concatenate(
                    [jnp.where(low, tq[:, cut], none), jnp.where(low, none, tq[:, cut])], axis=0
                ),
                tk[:, cut],
            )
            for cut in cuts
        ],
        axis=0,
    ).reshape(T_HEADS, 128, 128)
    scores = jnp.where(seen, scores, -jnp.inf)
    weights = jnp.exp(scores - jnp.max(scores, axis=-1, keepdims=True)).astype(BF16)
    gather(GATHER_AT[7])
    pieces = []
    for i, cut in enumerate(cuts):
        both = jnp.dot(
            weights[2 * i : 2 * i + 2].reshape(256, 128),
            jnp.concatenate([tv[:, cut], ones], axis=1),
            preferred_element_type=F32,
        )
        both = both[:, :128] / both[:, 128:]
        pieces.append(jnp.where(low, both[:128], both[128:]).astype(BF16))
    gather(GATHER_AT[8])
    time_heads = jnp.concatenate(pieces, axis=1)
    after_time = after_space + jnp.dot(time_heads, to[...], preferred_element_type=F32)
    gather(GATHER_AT[9])
    act_send[...] = layer_norm(after_time, gm_ref[...].reshape(1, D)).astype(BF16)

    act_copy = pair_copy(0, act_send, act_recv)
    act_copy.start()
    act_copy.wait_recv()
    act = jnp.concatenate([act_recv[...], act_send[...]], axis=0)
    partial = jnp.zeros((256, D), F32)
    for until, group_of in MLP_GROUPS:
        gather(until)
        w_in, w_out = [], []
        for p, steps in group_of:
            for step in steps:
                block = gathered[p][(me[ORDERS[p][2]] + step) % SIZE[ORDERS[p][2]]]
                w_in.append(block[:, 0].reshape(-1, D))
                w_out.append(block[:, 1].reshape(-1, D))
        hidden = gelu(nt_dot(act, jnp.concatenate(w_in, axis=0))).astype(BF16)
        partial += jnp.dot(hidden, jnp.concatenate(w_out, axis=0), preferred_element_type=F32)

    def red_copy(k):
        return pltpu.make_async_remote_copy(
            src_ref=red_send.at[(group + k) % 16], dst_ref=red_recv.at[k], send_sem=red_ss.at[k],
            recv_sem=red_rs.at[k], device_id=group_peer(k), device_id_type=MESH,
        )

    after_time = after_time + partial[128:]
    share = jnp.concatenate([partial[:128], after_time], axis=0).astype(BF16)
    vecs = nt_dot(cproj_ref[...], share)
    high = vecs.astype(BF16)
    rest = (vecs - high.astype(F32)).astype(BF16)
    sums = jnp.dot(
        jnp.concatenate([high, rest], axis=0), hot[...], preferred_element_type=F32
    )
    sums = sums[:32] + sums[32:]
    for dest in range(16):
        low_row, low_lane = dest // NZ * 16, dest % NZ * 128
        red_send[dest] = sums[low_row : low_row + 16, low_lane : low_lane + 128].astype(BF16)

    @pl.loop(1, 16)
    def _(k):
        red_copy(k).start()

    back_send[...] = partial[:128]
    back_copy = pair_copy(1, back_send, back_recv)
    back_copy.start()

    def tot_copy(k):
        return pltpu.make_async_remote_copy(
            src_ref=tot_all.at[f], dst_ref=tot_all.at[f], send_sem=tot_ss.at[k],
            recv_sem=tot_rs.at[k], device_id=frame_peer(k), device_id_type=MESH,
        )

    def mean_copy(k):
        return pltpu.make_async_remote_copy(
            src_ref=mean_send, dst_ref=mean_recv.at[group], send_sem=fin_ss.at[k],
            recv_sem=fin_rs.at[k], device_id=group_peer(k), device_id_type=MESH,
        )

    gather_sent()
    red_recv[0] = red_send[group]

    @pl.loop(1, 16)
    def _(k):
        red_copy(k).wait_recv()

    tot_all[f] = jnp.sum(red_recv[...].astype(F32), axis=0).astype(BF16)

    @pl.loop(1, 16)
    def _(k):
        tot_copy(k).start()

    back_copy.wait_recv()
    outputs = (after_time + back_recv[...]).reshape(FRAMES, 8, D)
    out_s[0] = outputs.astype(BF16)
    out_copy = pltpu.make_async_copy(out_s, out_hbm, load_sem.at[0])
    out_copy.start()
    for k in range(1, NZ):
        heads_copy(k).wait_send()
        count_copy(k).wait_send()
    for copy in (codes_copy, act_copy, back_copy):
        copy.wait_send()

    @pl.loop(1, 16)
    def _(k):
        rows_copy(k).wait_send()
        red_copy(k).wait_send()
        all_count_copy(k).wait_send()
        all_count_copy(k).wait_recv()

    counts = jnp.sum(count_all[...].astype(F32), axis=0)
    counts = jnp.maximum(counts[:8] + 256.0 * counts[8:], 1.0)
    counts = jnp.concatenate([counts, counts], axis=0)

    @pl.loop(1, 16)
    def _(k):
        tot_copy(k).wait_recv()

    means = (jnp.sum(tot_all[...].astype(F32), axis=0) / counts).astype(BF16)
    mean_send[...] = means
    mean_recv[group] = means

    @pl.loop(1, 16)
    def _(k):
        mean_copy(k).start()

    @pl.loop(1, 16)
    def _(k):
        tot_copy(k).wait_send()
        mean_copy(k).wait_send()

    out_copy.wait()

    @pl.loop(1, 16)
    def _(k):
        mean_copy(k).wait_recv()

    for g in range(16):
        cut = slice(g % NZ * 128, g % NZ * 128 + 128)
        means_ref[g // NZ * 16 : g // NZ * 16 + 16, cut] = mean_recv[g].astype(F32)


def shards(*args):
    args = list(args)
    args[2] = args[2].swapaxes(1, 2)
    args[10] = args[10].T
    args[11] = args[11].swapaxes(1, 2)
    args = [pltpu.with_memory_space_constraint(arg, pltpu.HBM) for arg in args]
    vmem = pl.BlockSpec(memory_space=pltpu.VMEM)
    hbm = pl.BlockSpec(memory_space=pltpu.HBM)
    dma = pltpu.SemaphoreType.DMA
    scratch = [
        pltpu.VMEM((POS, D), BF16),
        pltpu.VMEM((D,), F32),
        pltpu.VMEM((3, HD, D), BF16),
        pltpu.VMEM((512, D), BF16),
        pltpu.VMEM((D,), F32),
        pltpu.VMEM((3, D, D), BF16),
        pltpu.VMEM((D, D), BF16),
        pltpu.VMEM((D,), F32),
        pltpu.VMEM((24, D), BF16),
        pltpu.VMEM((24, D), BF16),
        pltpu.VMEM((32, D), BF16),
        pltpu.VMEM((1, 8, FRAMES), jnp.int32),
        pltpu.VMEM((NZ, 128, 128), BF16),
        pltpu.VMEM((POS, 128), BF16),
        pltpu.VMEM((POS, 128), BF16),
        pltpu.VMEM((NZ, 64, 128), BF16),
        pltpu.VMEM((NZ, 64, 128), BF16),
        pltpu.VMEM((FRAMES, 16, HALF), BF16),
        pltpu.VMEM((FRAMES, 16, HALF), BF16),
        pltpu.VMEM((3, 16, D), BF16),
    ]
    scratch += [pltpu.VMEM((SIZE[order[0]] // 2, 16, D), BF16) for order in ORDERS]
    scratch += [
        pltpu.VMEM((SIZE[order[2]], SIZE[order[1]], 2, units, D), BF16)
        for order, units in zip(ORDERS, UNITS)
    ]
    scratch += [
        pltpu.VMEM((1, 8, FRAMES), jnp.int32),
        pltpu.VMEM((256, CODES), BF16),
        pltpu.VMEM((NZ, 16, 128), BF16),
        pltpu.VMEM((NZ, 16, 128), BF16),
        pltpu.VMEM((FRAMES, 16, 128), BF16),
        pltpu.VMEM((128, D), BF16),
        pltpu.VMEM((128, D), BF16),
        pltpu.VMEM((128, D), F32),
        pltpu.VMEM((128, D), F32),
        pltpu.VMEM((1, FRAMES, 8, D), BF16),
        pltpu.VMEM((16, 16, 128), BF16),
        pltpu.VMEM((16, 16, 128), BF16),
        pltpu.VMEM((FRAMES, 16, 128), BF16),
        pltpu.VMEM((16, 128), BF16),
        pltpu.VMEM((16, 16, 128), BF16),
    ]
    scratch += [
        dma((12,)),
        dma((NZ,)), dma((NZ,)),
        dma((FRAMES,)), dma((FRAMES,)),
        dma((3, NZ)), dma((3, NZ)),
        dma((3, 4)), dma((3, 4)),
        dma((3, 4, 4, 2)), dma((3, 4, 4, 2)),
        dma((3,)), dma((3,)),
        dma((16,)), dma((16,)),
        dma((16,)), dma((16,)),
        dma((16,)), dma((16,)),
        dma((NZ,)), dma((NZ,)),
        dma((16,)), dma((16,)),
    ]
    block_out, means = pl.pallas_call(
        block_kernel,
        out_shape=(
            jax.ShapeDtypeStruct((1, FRAMES, 8, D), BF16),
            jax.ShapeDtypeStruct((32, CODES), F32),
        ),
        in_specs=[hbm] * 12,
        out_specs=(hbm, vmem),
        scratch_shapes=scratch,
        compiler_params=pltpu.CompilerParams(
            collective_id=0, has_side_effects=True, vmem_limit_bytes=52 * 1024 * 1024
        ),
    )(*args)
    return block_out, means.T


def solution(mesh):
    placed = (
        P("dp", "frame", None, None),
        P(),
        P(None, None, "mp"),
        P(),
        P(),
        P(),
        P(),
        P(),
        P(("frame", "mp"), None),
        P(("frame", "mp"), None),
        P(),
        P("dp", None, ("frame", "mp")),
    )
    return jax.shard_map(
        shards,
        mesh=mesh,
        in_specs=placed,
        out_specs=(P("dp", None, ("frame", "mp"), None), P()),
        check_vma=False,
    )
```

```python
import math

import jax
import jax.numpy as jnp
from jax import lax
from jax.experimental import pallas as pl
from jax.experimental.pallas import tpu as pltpu
from jax.sharding import PartitionSpec as P

F32 = jnp.float32
BF16 = jnp.bfloat16
MESH = pl.DeviceIdType.MESH

D = 768
HALF = D // 2
HD = 64
T_HEADS = 12
CODES = 1024
POS = 1024
FRAMES = 16
NX, NY, NZ = 4, 4, 8
SIZE = {"x": NX, "y": NY, "z": NZ}
ORDERS = (("x", "y", "z"), ("z", "y", "x"), ("z", "x", "y"))
UNITS = tuple(SIZE[order[0]] // 2 * 8 for order in ORDERS)
EVENTS = (
    (0, 0), (1, 0), (0, 1, 1), (2, 0), (0, 1, 3), (0, 1, 2),
    (0, 2, 1, 0), (1, 2, 1, 0), (1, 1, 1),
    (0, 2, 1, 1), (2, 1, 1), (1, 1, 3), (1, 1, 2), (0, 2, 1, 3),
    (0, 2, 1, 2), (2, 1, 3), (2, 1, 2), (2, 2, 1, 0),
    (0, 2, 2, 0), (0, 2, 2, 1), (0, 2, 2, 3), (1, 2, 2, 0),
    (0, 2, 2, 2), (2, 2, 1, 1), (0, 2, 3, 0), (1, 2, 1, 1),
    (0, 2, 3, 1), (2, 2, 1, 3), (0, 2, 3, 3), (1, 2, 1, 3),
    (0, 2, 3, 2), (2, 2, 1, 2), (1, 2, 1, 2),
    (2, 2, 2, 0), (0, 2, 4, 0), (0, 2, 4, 1), (1, 2, 2, 1), (2, 2, 2, 1),
    (0, 2, 4, 3), (1, 2, 2, 3), (0, 2, 4, 2), (2, 2, 2, 3), (1, 2, 2, 2), (2, 2, 2, 2),
)
GATHER_AT = (0, 1, 1, 1, 6, 23, 24, 27, 28, 29)
MLP_GROUPS = (
    (29, ((0, (0, 1, 7, 2)),)),
    (32, ((2, (0, 1)),)),
    (33, ((1, (0, 1)),)),
    (33, ((0, (6, 3, 5)), (1, (3,)))),
    (41, ((2, (3,)), (0, (4,)))),
    (44, ((1, (2,)), (2, (2,)))),
)
FRAME_ORDER = sorted(range(1, 16), key=lambda k: -min(k // 4, 4 - k // 4) - min(k % 4, 4 - k % 4))
GROUP_ORDER = sorted(range(1, 16), key=lambda k: -min(k % 8, 8 - k % 8))
SOURCES = {"x": ((0, 1), (2, 3)), "z": ((0, 1), (2, 7), (6, 3), (4, 5))}


def layer_norm(values, gain):
    center = jnp.mean(values, axis=-1, keepdims=True)
    shifted = values - center
    spread = jnp.mean(shifted * shifted, axis=-1, keepdims=True)
    return shifted * lax.rsqrt(spread + 1e-06) * gain


def nt_dot(a, b):
    return lax.dot_general(a, b, (((1,), (1,)), ((), ())), preferred_element_type=F32)


def gelu(v):
    inner = math.sqrt(2.0 / math.pi) * (v + 0.044715 * (v * v * v))
    return 0.5 * v * (1.0 + jnp.tanh(inner))


def lanes(shape):
    return lax.broadcasted_iota(jnp.int32, shape, len(shape) - 1)


def block_kernel(
    frames_hbm, gs_hbm, sproj_hbm, sout_hbm, gt_hbm, tproj_hbm, tout_hbm, gm_hbm,
    win_hbm, wout_hbm, cproj_hbm, cidx_hbm,
    out_hbm, means_ref,
    fr, gs_ref, sp, so, gt_ref, tp, to, gm_ref, win_ref, wout_ref, cproj_ref, cidx_ref,
    q_s, k_s, v_s,
    heads_send, heads_recv, rows_send, rows_recv,
    own_parts, first0, first1, first2, w0, w1, w2,
    cidx_recv, hot, count_send, count_recv, count_all,
    act_send, act_recv, back_send, back_recv,
    out_s, red_send, red_recv, tot_all, mean_send, mean_recv,
    load_sem, heads_ss, heads_rs, rows_ss, rows_rs, first_ss, first_rs,
    second_ss, second_rs,    ring_ss, ring_rs, pair_ss, pair_rs, red_ss, red_rs, tot_ss, tot_rs, fin_ss, fin_rs,
    count_ss, count_rs, all_count_ss, all_count_rs,
):
    c = lax.axis_index("dp")
    f = lax.axis_index("frame")
    m = lax.axis_index("mp")
    me = {"x": f // NY, "y": f % NY, "z": m}
    group = c * NZ + m

    def at(**moved):
        x = moved.get("x", me["x"])
        y = moved.get("y", me["y"])
        return (c, x * NY + y, moved.get("z", m))

    def frame_peer(k):
        return at(x=(me["x"] + k // NY) % NX, y=(me["y"] + k % NY) % NY)

    def group_peer(k):
        return ((c + k // NZ) % 2, f, (m + k % NZ) % NZ)

    barrier = pltpu.get_barrier_semaphore()

    for k in GROUP_ORDER:
        pl.semaphore_signal(barrier, inc=1, device_id=group_peer(k), device_id_type=MESH)
    for k in FRAME_ORDER:
        pl.semaphore_signal(barrier, inc=1, device_id=frame_peer(k), device_id_type=MESH)

    loads = {}
    for name, src, dst in (
        ("win", win_hbm, win_ref), ("wout", wout_hbm, wout_ref),
        ("gs", gs_hbm, gs_ref), ("sp", sproj_hbm, sp), ("fr", frames_hbm.at[0, 0], fr),
        ("so", sout_hbm, so), ("gt", gt_hbm, gt_ref), ("tp", tproj_hbm, tp),
        ("to", tout_hbm, to), ("gm", gm_hbm, gm_ref),
        ("cproj", cproj_hbm, cproj_ref), ("cidx", cidx_hbm, cidx_ref),
    ):
        loads[name] = pltpu.make_async_copy(src, dst, load_sem.at[len(loads)])
        loads[name].start()
    loads["win"].wait()
    loads["wout"].wait()

    win = win_ref[...].astype(F32)
    wout = wout_ref[...].astype(F32)
    for p in range(3):
        own_parts[p] = jnp.concatenate(
            [win[p * 8 : p * 8 + 8], wout[p * 8 : p * 8 + 8]], axis=0
        ).astype(BF16)
    firsts = (first0, first1, first2)
    gathered = (w0, w1, w2)

    def first_copy(p, slot):
        axis = ORDERS[p][0]
        zero, one = SOURCES[axis][slot]
        back = SIZE[axis] - zero - c * (one - zero)
        return pltpu.make_async_remote_copy(
            src_ref=own_parts.at[p], dst_ref=firsts[p].at[slot],
            send_sem=first_ss.at[p, slot], recv_sem=first_rs.at[p, slot],
            device_id=at(**{axis: (me[axis] + back) % SIZE[axis]}), device_id_type=MESH,
        )

    def first_send(p):
        for slot in range(1, len(SOURCES[ORDERS[p][0]])):
            first_copy(p, slot).start()

        @pl.when(c == 1)
        def _():
            first_copy(p, 0).start()

        @pl.when(c == 0)
        def _():
            firsts[p][0] = own_parts[p]

    def first_wait(p):
        n = SIZE[ORDERS[p][0]]
        for slot in range(1, n // 2):
            first_copy(p, slot).wait_recv()

        @pl.when(c == 1)
        def _():
            first_copy(p, 0).wait_recv()

        block = firsts[p][...].astype(F32).reshape(n // 2, 2, 8, D)
        at3, at2 = me[ORDERS[p][2]], me[ORDERS[p][1]]
        for side in range(2):
            gathered[p][at3, at2, side] = block[:, side].reshape(n // 2 * 8, D).astype(BF16)

    def first_done(p):
        for slot in range(1, len(SOURCES[ORDERS[p][0]])):
            first_copy(p, slot).wait_send()

        @pl.when(c == 1)
        def _():
            first_copy(p, 0).wait_send()

    def second_copy(p, k):
        _, axis, last = ORDERS[p]
        block = gathered[p].at[me[last], me[axis]]
        return pltpu.make_async_remote_copy(
            src_ref=block, dst_ref=block,
            send_sem=second_ss.at[p, k], recv_sem=second_rs.at[p, k],
            device_id=at(**{axis: (me[axis] + k) % SIZE[axis]}), device_id_type=MESH,
        )

    def ring_copy(p, step, sub, way):
        _, inner, axis = ORDERS[p]
        n = SIZE[axis]
        shift = (n - (step - 1)) if way == 0 else (step - 1)
        block = gathered[p].at[
            (me[axis] + shift) % n, (me[inner] + SIZE[inner] - sub) % SIZE[inner]
        ]
        if step == n // 2:
            block = block.at[way]
        return pltpu.make_async_remote_copy(
            src_ref=block, dst_ref=block,
            send_sem=ring_ss.at[p, step - 1, sub, way],
            recv_sem=ring_rs.at[p, step - 1, sub, way],
            device_id=at(**{axis: (me[axis] + (1 if way == 0 else n - 1)) % n}),
            device_id_type=MESH,
        )

    def ring_send(p, step, sub):
        if step <= SIZE[ORDERS[p][2]] // 2:
            for way in range(2):
                ring_copy(p, step, sub, way).start()

    todo = list(EVENTS)

    def gather(until):
        count = until - len(EVENTS) + len(todo)
        for event in todo[:count]:
            p = event[0]
            if event[1] == 0:
                first_wait(p)
                for k in (1, 3, 2):
                    second_copy(p, k).start()
                ring_send(p, 1, 0)
            elif event[1] == 1:
                second_copy(p, event[2]).wait_recv()
                ring_send(p, 1, event[2])
            else:
                for way in range(2):
                    ring_copy(p, event[2], event[3], way).wait_recv()
                ring_send(p, event[2] + 1, event[3])
        del todo[:count]

    def gather_sent():
        for p in range(3):
            first_done(p)
            for k in range(1, 4):
                second_copy(p, k).wait_send()
            for step in range(1, SIZE[ORDERS[p][2]] // 2 + 1):
                for sub in range(4):
                    for way in range(2):
                        ring_copy(p, step, sub, way).wait_send()

    partner = (1 - c, f, m)

    def pair_copy(i, src, dst):
        return pltpu.make_async_remote_copy(
            src_ref=src, dst_ref=dst, send_sem=pair_ss.at[i], recv_sem=pair_rs.at[i],
            device_id=partner, device_id_type=MESH,
        )

    loads["cidx"].wait()
    pl.semaphore_wait(barrier, 30)
    for p in range(3):
        first_send(p)
    codes_copy = pair_copy(2, cidx_ref, cidx_recv)
    codes_copy.start()

    for name in ("gs", "sp", "fr"):
        loads[name].wait()
    wqkv = jnp.concatenate([sp[...].reshape(3 * HD, D), jnp.zeros((HD, D), BF16)], axis=0)
    gain_space = gs_ref[...].reshape(1, D)

    @pl.loop(0, 4)
    def _(i):
        rows = pl.ds(pl.multiple_of(i * 256, 256), 256)
        normed = layer_norm(fr[rows, :].astype(F32), gain_space).astype(BF16)
        both = nt_dot(normed, wqkv)
        qk = both[:, :128]
        low = lanes((256, 128)) < HD
        k_s[rows, :] = pltpu.roll(qk, HD, 1).astype(BF16)
        v = both[:, 128:]
        v_s[rows, :] = jnp.where(low, v, 1.0).astype(BF16)
        q = jnp.where(low, qk * (1.0 / math.sqrt(HD)), 0.0).reshape(4, NZ, 8, 128)
        for to_m in range(NZ):
            q_s[to_m, pl.ds(pl.multiple_of(i * 32, 32), 32), :] = (
                q[:, to_m].reshape(32, 128).astype(BF16)
            )

    def heads_copy(shift):
        dest = (m + shift) % NZ
        return pltpu.make_async_remote_copy(
            src_ref=heads_send.at[dest], dst_ref=heads_recv.at[m],
            send_sem=heads_ss.at[shift], recv_sem=heads_rs.at[shift],
            device_id=(c, f, dest), device_id_type=MESH,
        )

    half = lanes((64, 128)) < HD
    for i, shifts in enumerate(((4, 3), (5, 2), (6, 1), (7, 0))):
        queries = jnp.concatenate([q_s[(m + shift) % NZ] for shift in shifts], axis=0)
        scores = nt_dot(queries, k_s[...])
        weights = jnp.exp(scores - jnp.max(scores, axis=-1, keepdims=True)).astype(BF16)
        mixed = jnp.dot(weights, v_s[...], preferred_element_type=F32)
        turned = pltpu.roll(mixed, HD, 1)
        for j, shift in enumerate(shifts):
            top, bottom = slice(j * 128, j * 128 + 64), slice(j * 128 + 64, j * 128 + 128)
            heads_send[(m + shift) % NZ] = (
                jnp.where(half, mixed[top], turned[bottom])
                / jnp.where(half, turned[top], mixed[bottom])
            ).astype(BF16)
        for shift in shifts:
            if shift:
                heads_copy(shift).start()
        gather(GATHER_AT[i])

    heads_recv[m] = heads_send[m]

    def onehot(codes):
        codes = jnp.broadcast_to(codes, (FRAMES, 8, FRAMES)).reshape(128, FRAMES)
        diagonal = lax.broadcasted_iota(jnp.int32, (128, FRAMES), 0) // 8 == lanes((128, FRAMES))
        codes = jnp.sum(jnp.where(diagonal, codes, 0), axis=1, keepdims=True)
        return (codes == lanes((128, CODES))).astype(F32).astype(BF16)

    def count_copy(k):
        dest = (m + k) % NZ
        return pltpu.make_async_remote_copy(
            src_ref=count_send.at[dest], dst_ref=count_recv.at[k], send_sem=count_ss.at[k],
            recv_sem=count_rs.at[k], device_id=(c, f, dest), device_id_type=MESH,
        )

    def all_count_copy(k):
        return pltpu.make_async_remote_copy(
            src_ref=count_all.at[f], dst_ref=count_all.at[f], send_sem=all_count_ss.at[k],
            recv_sem=all_count_rs.at[k], device_id=frame_peer(k), device_id_type=MESH,
        )

    codes_copy.wait_recv()
    hot[:128] = onehot(cidx_recv[...])
    hot[128:] = onehot(cidx_ref[...])
    counts = jnp.dot(jnp.ones((16, 256), BF16), hot[...], preferred_element_type=F32)
    for dest in range(NZ):
        count_send[dest] = counts[:, dest * 128 : dest * 128 + 128].astype(BF16)
    for k in range(1, NZ):
        count_copy(k).start()
    count_recv[0] = count_send[m]
    gather(GATHER_AT[4])
    for k in range(1, NZ):
        heads_copy(k).wait_recv()

    side = lanes((64, 128)) < HD
    upper, lower = [], []
    for i in range(NZ // 2):
        even = heads_recv[2 * i].astype(F32)
        odd = heads_recv[2 * i + 1].astype(F32)
        upper.append(jnp.where(side, even, pltpu.roll(odd, HD, 1)))
        lower.append(jnp.where(side, pltpu.roll(even, HD, 1), odd))
    heads_all = jnp.concatenate(
        [jnp.concatenate(upper, axis=1), jnp.concatenate(lower, axis=1)], axis=0
    ).astype(BF16)
    own = []
    for i in range(FRAMES):
        pair = fr[pl.ds(pl.multiple_of(i * 64 + (m // 2) * 16, 16), 16), :].astype(F32)
        own.append(jnp.where(m % 2 == 0, pair[:8], pair[8:]))
    loads["so"].wait()
    after_space = jnp.concatenate(own, axis=0) + jnp.dot(
        heads_all, so[...], preferred_element_type=F32
    )
    split = after_space.reshape(FRAMES, 8, D)
    rows_send[...] = jnp.concatenate([split[:, :, :HALF], split[:, :, HALF:]], axis=1).astype(BF16)

    def rows_copy(k):
        peer = frame_peer(k)
        return pltpu.make_async_remote_copy(
            src_ref=rows_send.at[peer[1]], dst_ref=rows_recv.at[f],
            send_sem=rows_ss.at[k], recv_sem=rows_rs.at[k],
            device_id=peer, device_id_type=MESH,
        )

    for k in FRAME_ORDER:
        rows_copy(k).start()

    rows_recv[f] = rows_send[f]
    for k in range(1, NZ):
        count_copy(k).wait_recv()
    counts = jnp.sum(count_recv[...].astype(F32), axis=0)
    upper = jnp.floor(counts[:8] * (1.0 / 256.0))
    count_all[f] = jnp.concatenate([counts[8:] - 256.0 * upper, upper], axis=0).astype(BF16)

    for k in FRAME_ORDER:
        all_count_copy(k).start()

    gather(GATHER_AT[5])

    @pl.loop(1, FRAMES)
    def _(k):
        rows_copy(k).wait_recv()

    for name in ("gt", "tp", "to", "gm", "cproj"):
        loads[name].wait()
    arrived = rows_recv[...].astype(F32)
    after_space = jnp.concatenate([arrived[:, :8], arrived[:, 8:]], axis=2).reshape(128, D)
    time_in = layer_norm(after_space, gt_ref[...].reshape(1, D)).astype(BF16)
    tq = jnp.dot(time_in, tp[0], preferred_element_type=F32) * (1.0 / math.sqrt(HD))
    tk = jnp.dot(time_in, tp[1], preferred_element_type=F32).astype(BF16)
    tv = jnp.dot(time_in, tp[2], preferred_element_type=F32).astype(BF16)
    tq = tq.astype(BF16)
    gather(GATHER_AT[6])
    row = lax.broadcasted_iota(jnp.int32, (128, 128), 0)
    col = lax.broadcasted_iota(jnp.int32, (128, 128), 1)
    seen = ((row % 8 == col % 8) & (col // 8 <= row // 8))[None]
    low = col < HD
    none = jnp.zeros((128, 128), BF16)
    ones = jnp.ones((128, 128), BF16)
    cuts = [slice(i * 128, i * 128 + 128) for i in range(T_HEADS // 2)]
    scores = jnp.concatenate(
        [
            nt_dot(
                jnp.concatenate(
                    [jnp.where(low, tq[:, cut], none), jnp.where(low, none, tq[:, cut])], axis=0
                ),
                tk[:, cut],
            )
            for cut in cuts
        ],
        axis=0,
    ).reshape(T_HEADS, 128, 128)
    scores = jnp.where(seen, scores, -jnp.inf)
    weights = jnp.exp(scores - jnp.max(scores, axis=-1, keepdims=True)).astype(BF16)
    gather(GATHER_AT[7])
    pieces = []
    for i, cut in enumerate(cuts):
        both = jnp.dot(
            weights[2 * i : 2 * i + 2].reshape(256, 128),
            jnp.concatenate([tv[:, cut], ones], axis=1),
            preferred_element_type=F32,
        )
        both = both[:, :128] / both[:, 128:]
        pieces.append(jnp.where(low, both[:128], both[128:]).astype(BF16))
    gather(GATHER_AT[8])
    time_heads = jnp.concatenate(pieces, axis=1)
    after_time = after_space + jnp.dot(time_heads, to[...], preferred_element_type=F32)
    gather(GATHER_AT[9])
    act_send[...] = layer_norm(after_time, gm_ref[...].reshape(1, D)).astype(BF16)

    act_copy = pair_copy(0, act_send, act_recv)
    act_copy.start()
    act_copy.wait_recv()
    act = jnp.concatenate([act_recv[...], act_send[...]], axis=0)
    partial = jnp.zeros((256, D), F32)
    for until, group_of in MLP_GROUPS:
        gather(until)
        w_in, w_out = [], []
        for p, steps in group_of:
            for step in steps:
                block = gathered[p][(me[ORDERS[p][2]] + step) % SIZE[ORDERS[p][2]]]
                w_in.append(block[:, 0].reshape(-1, D))
                w_out.append(block[:, 1].reshape(-1, D))
        hidden = gelu(nt_dot(act, jnp.concatenate(w_in, axis=0))).astype(BF16)
        partial += jnp.dot(hidden, jnp.concatenate(w_out, axis=0), preferred_element_type=F32)

    def red_copy(k):
        peer = group_peer(k)
        return pltpu.make_async_remote_copy(
            src_ref=red_send.at[peer[0] * NZ + peer[2]], dst_ref=red_recv.at[k],
            send_sem=red_ss.at[k], recv_sem=red_rs.at[k], device_id=peer, device_id_type=MESH,
        )

    after_time = after_time + partial[128:]
    share = jnp.concatenate([partial[:128], after_time], axis=0).astype(BF16)
    vecs = nt_dot(cproj_ref[...], share)
    high = vecs.astype(BF16)
    rest = (vecs - high.astype(F32)).astype(BF16)
    sums = jnp.dot(
        jnp.concatenate([high, rest], axis=0), hot[...], preferred_element_type=F32
    )
    sums = sums[:32] + sums[32:]
    for dest in range(16):
        low_row, low_lane = dest // NZ * 16, dest % NZ * 128
        red_send[dest] = sums[low_row : low_row + 16, low_lane : low_lane + 128].astype(BF16)

    for k in GROUP_ORDER:
        red_copy(k).start()

    back_send[...] = partial[:128]
    back_copy = pair_copy(1, back_send, back_recv)
    back_copy.start()

    def tot_copy(k):
        return pltpu.make_async_remote_copy(
            src_ref=tot_all.at[f], dst_ref=tot_all.at[f], send_sem=tot_ss.at[k],
            recv_sem=tot_rs.at[k], device_id=frame_peer(k), device_id_type=MESH,
        )

    def mean_copy(k):
        return pltpu.make_async_remote_copy(
            src_ref=mean_send, dst_ref=mean_recv.at[group], send_sem=fin_ss.at[k],
            recv_sem=fin_rs.at[k], device_id=group_peer(k), device_id_type=MESH,
        )

    gather_sent()
    red_recv[0] = red_send[group]

    @pl.loop(1, 16)
    def _(k):
        red_copy(k).wait_recv()

    tot_all[f] = jnp.sum(red_recv[...].astype(F32), axis=0).astype(BF16)

    for k in FRAME_ORDER:
        tot_copy(k).start()

    back_copy.wait_recv()
    outputs = (after_time + back_recv[...]).reshape(FRAMES, 8, D)
    out_s[0] = outputs.astype(BF16)
    out_copy = pltpu.make_async_copy(out_s, out_hbm, load_sem.at[0])
    out_copy.start()
    for k in range(1, NZ):
        heads_copy(k).wait_send()
        count_copy(k).wait_send()
    for copy in (codes_copy, act_copy, back_copy):
        copy.wait_send()

    @pl.loop(1, 16)
    def _(k):
        rows_copy(k).wait_send()
        red_copy(k).wait_send()
        all_count_copy(k).wait_send()
        all_count_copy(k).wait_recv()

    counts = jnp.sum(count_all[...].astype(F32), axis=0)
    counts = jnp.maximum(counts[:8] + 256.0 * counts[8:], 1.0)
    counts = jnp.concatenate([counts, counts], axis=0)

    @pl.loop(1, 16)
    def _(k):
        tot_copy(k).wait_recv()

    means = (jnp.sum(tot_all[...].astype(F32), axis=0) / counts).astype(BF16)
    mean_send[...] = means
    mean_recv[group] = means

    for k in GROUP_ORDER:
        mean_copy(k).start()

    @pl.loop(1, 16)
    def _(k):
        tot_copy(k).wait_send()
        mean_copy(k).wait_send()

    out_copy.wait()

    @pl.loop(1, 16)
    def _(k):
        mean_copy(k).wait_recv()

    for g in range(16):
        cut = slice(g % NZ * 128, g % NZ * 128 + 128)
        means_ref[g // NZ * 16 : g // NZ * 16 + 16, cut] = mean_recv[g].astype(F32)


def shards(*args):
    args = list(args)
    args[2] = args[2].swapaxes(1, 2)
    args[10] = args[10].T
    args[11] = args[11].swapaxes(1, 2)
    args = [pltpu.with_memory_space_constraint(arg, pltpu.HBM) for arg in args]
    vmem = pl.BlockSpec(memory_space=pltpu.VMEM)
    hbm = pl.BlockSpec(memory_space=pltpu.HBM)
    dma = pltpu.SemaphoreType.DMA
    scratch = [
        pltpu.VMEM((POS, D), BF16),
        pltpu.VMEM((D,), F32),
        pltpu.VMEM((3, HD, D), BF16),
        pltpu.VMEM((512, D), BF16),
        pltpu.VMEM((D,), F32),
        pltpu.VMEM((3, D, D), BF16),
        pltpu.VMEM((D, D), BF16),
        pltpu.VMEM((D,), F32),
        pltpu.VMEM((24, D), BF16),
        pltpu.VMEM((24, D), BF16),
        pltpu.VMEM((32, D), BF16),
        pltpu.VMEM((1, 8, FRAMES), jnp.int32),
        pltpu.VMEM((NZ, 128, 128), BF16),
        pltpu.VMEM((POS, 128), BF16),
        pltpu.VMEM((POS, 128), BF16),
        pltpu.VMEM((NZ, 64, 128), BF16),
        pltpu.VMEM((NZ, 64, 128), BF16),
        pltpu.VMEM((FRAMES, 16, HALF), BF16),
        pltpu.VMEM((FRAMES, 16, HALF), BF16),
        pltpu.VMEM((3, 16, D), BF16),
    ]
    scratch += [pltpu.VMEM((SIZE[order[0]] // 2, 16, D), BF16) for order in ORDERS]
    scratch += [
        pltpu.VMEM((SIZE[order[2]], SIZE[order[1]], 2, units, D), BF16)
        for order, units in zip(ORDERS, UNITS)
    ]
    scratch += [
        pltpu.VMEM((1, 8, FRAMES), jnp.int32),
        pltpu.VMEM((256, CODES), BF16),
        pltpu.VMEM((NZ, 16, 128), BF16),
        pltpu.VMEM((NZ, 16, 128), BF16),
        pltpu.VMEM((FRAMES, 16, 128), BF16),
        pltpu.VMEM((128, D), BF16),
        pltpu.VMEM((128, D), BF16),
        pltpu.VMEM((128, D), F32),
        pltpu.VMEM((128, D), F32),
        pltpu.VMEM((1, FRAMES, 8, D), BF16),
        pltpu.VMEM((16, 16, 128), BF16),
        pltpu.VMEM((16, 16, 128), BF16),
        pltpu.VMEM((FRAMES, 16, 128), BF16),
        pltpu.VMEM((16, 128), BF16),
        pltpu.VMEM((16, 16, 128), BF16),
    ]
    scratch += [
        dma((12,)),
        dma((NZ,)), dma((NZ,)),
        dma((FRAMES,)), dma((FRAMES,)),
        dma((3, NZ)), dma((3, NZ)),
        dma((3, 4)), dma((3, 4)),
        dma((3, 4, 4, 2)), dma((3, 4, 4, 2)),
        dma((3,)), dma((3,)),
        dma((16,)), dma((16,)),
        dma((16,)), dma((16,)),
        dma((16,)), dma((16,)),
        dma((NZ,)), dma((NZ,)),
        dma((16,)), dma((16,)),
    ]
    block_out, means = pl.pallas_call(
        block_kernel,
        out_shape=(
            jax.ShapeDtypeStruct((1, FRAMES, 8, D), BF16),
            jax.ShapeDtypeStruct((32, CODES), F32),
        ),
        in_specs=[hbm] * 12,
        out_specs=(hbm, vmem),
        scratch_shapes=scratch,
        compiler_params=pltpu.CompilerParams(
            collective_id=0, has_side_effects=True, vmem_limit_bytes=52 * 1024 * 1024
        ),
    )(*args)
    return block_out, means.T


def solution(mesh):
    placed = (
        P("dp", "frame", None, None),
        P(),
        P(None, None, "mp"),
        P(),
        P(),
        P(),
        P(),
        P(),
        P(("frame", "mp"), None),
        P(("frame", "mp"), None),
        P(),
        P("dp", None, ("frame", "mp")),
    )
    return jax.shard_map(
        shards,
        mesh=mesh,
        in_specs=placed,
        out_specs=(P("dp", None, ("frame", "mp"), None), P()),
        check_vma=False,
    )
```

```python
import math

import jax
import jax.numpy as jnp
from jax import lax
from jax.experimental import pallas as pl
from jax.experimental.pallas import tpu as pltpu
from jax.sharding import PartitionSpec as P

F32 = jnp.float32
BF16 = jnp.bfloat16
MESH = pl.DeviceIdType.MESH

D = 768
HALF = D // 2
HD = 64
T_HEADS = 12
CODES = 1024
POS = 1024
FRAMES = 16
NX, NY, NZ = 4, 4, 8
SIZE = {"x": NX, "y": NY, "z": NZ}
ORDERS = (("x", "y", "z"), ("z", "y", "x"), ("z", "x", "y"))
UNITS = tuple(SIZE[order[0]] // 2 * 8 for order in ORDERS)
EVENTS = (
    (0, 0), (1, 0), (0, 1, 1), (2, 0), (0, 1, 3), (0, 1, 2),
    (0, 2, 1, 0), (1, 2, 1, 0), (1, 1, 1),
    (0, 2, 1, 1), (2, 1, 1), (1, 1, 3), (1, 1, 2), (0, 2, 1, 3),
    (0, 2, 1, 2), (2, 1, 3), (2, 1, 2), (2, 2, 1, 0),
    (0, 2, 2, 0), (0, 2, 2, 1), (0, 2, 2, 3), (1, 2, 2, 0),
    (0, 2, 2, 2), (2, 2, 1, 1), (0, 2, 3, 0), (1, 2, 1, 1),
    (0, 2, 3, 1), (2, 2, 1, 3), (0, 2, 3, 3), (1, 2, 1, 3),
    (0, 2, 3, 2), (2, 2, 1, 2), (1, 2, 1, 2),
    (2, 2, 2, 0), (0, 2, 4, 0), (0, 2, 4, 1), (1, 2, 2, 1), (2, 2, 2, 1),
    (0, 2, 4, 3), (1, 2, 2, 3), (0, 2, 4, 2), (2, 2, 2, 3), (1, 2, 2, 2), (2, 2, 2, 2),
)
GATHER_AT = (0, 1, 1, 1, 6, 23, 24, 27, 28, 29)
MLP_GROUPS = (
    (29, ((0, (0, 1, 7, 2)),)),
    (32, ((2, (0, 1)),)),
    (33, ((1, (0, 1)),)),
    (33, ((0, (6, 3, 5)), (1, (3,)))),
    (41, ((2, (3,)), (0, (4,)))),
    (44, ((1, (2,)), (2, (2,)))),
)
FRAME_ORDER = sorted(range(1, 16), key=lambda k: -min(k // 4, 4 - k // 4) - min(k % 4, 4 - k % 4))
GROUP_ORDER = sorted(range(1, 16), key=lambda k: -min(k % 8, 8 - k % 8))
SOURCES = {"x": ((0, 1), (2, 3)), "z": ((0, 1), (2, 7), (6, 3), (4, 5))}


def layer_norm(values, gain):
    center = jnp.mean(values, axis=-1, keepdims=True)
    shifted = values - center
    spread = jnp.mean(shifted * shifted, axis=-1, keepdims=True)
    return shifted * lax.rsqrt(spread + 1e-06) * gain


def nt_dot(a, b):
    return lax.dot_general(a, b, (((1,), (1,)), ((), ())), preferred_element_type=F32)


def gelu(v):
    inner = math.sqrt(2.0 / math.pi) * (v + 0.044715 * (v * v * v))
    return 0.5 * v * (1.0 + jnp.tanh(inner))


def lanes(shape):
    return lax.broadcasted_iota(jnp.int32, shape, len(shape) - 1)


def block_kernel(
    frames_hbm, gs_hbm, sproj_hbm, sout_hbm, gt_hbm, tproj_hbm, tout_hbm, gm_hbm,
    win_hbm, wout_hbm, cproj_hbm, cidx_hbm,
    out_hbm, means_ref,
    fr, gs_ref, sp, so, gt_ref, tp, to, gm_ref, win_ref, wout_ref, cproj_ref, cidx_ref,
    q_s, k_s, v_s,
    heads_send, heads_recv, rows_send, rows_recv,
    own_parts, first0, first1, first2, w0, w1, w2,
    cidx_recv, hot, count_send, count_recv, count_all,
    act_send, act_recv, back_send, back_recv,
    out_s, red_send, red_recv, tot_all, mean_send, mean_recv,
    load_sem, heads_ss, heads_rs, rows_ss, rows_rs, first_ss, first_rs,
    second_ss, second_rs,    ring_ss, ring_rs, pair_ss, pair_rs, red_ss, red_rs, tot_ss, tot_rs, fin_ss, fin_rs,
    count_ss, count_rs, all_count_ss, all_count_rs,
):
    c = lax.axis_index("dp")
    f = lax.axis_index("frame")
    m = lax.axis_index("mp")
    me = {"x": f // NY, "y": f % NY, "z": m}
    group = c * NZ + m

    def at(**moved):
        x = moved.get("x", me["x"])
        y = moved.get("y", me["y"])
        return (c, x * NY + y, moved.get("z", m))

    def frame_peer(k):
        return at(x=(me["x"] + k // NY) % NX, y=(me["y"] + k % NY) % NY)

    def group_peer(k):
        return ((c + k // NZ) % 2, f, (m + k % NZ) % NZ)

    barrier = pltpu.get_barrier_semaphore()

    for k in GROUP_ORDER:
        pl.semaphore_signal(barrier, inc=1, device_id=group_peer(k), device_id_type=MESH)
    for k in FRAME_ORDER:
        pl.semaphore_signal(barrier, inc=1, device_id=frame_peer(k), device_id_type=MESH)

    loads = {}
    for name, src, dst in (
        ("win", win_hbm, win_ref), ("wout", wout_hbm, wout_ref),
        ("gs", gs_hbm, gs_ref), ("sp", sproj_hbm, sp), ("fr", frames_hbm.at[0, 0], fr),
        ("so", sout_hbm, so), ("gt", gt_hbm, gt_ref), ("tp", tproj_hbm, tp),
        ("to", tout_hbm, to), ("gm", gm_hbm, gm_ref),
        ("cproj", cproj_hbm, cproj_ref), ("cidx", cidx_hbm, cidx_ref),
    ):
        loads[name] = pltpu.make_async_copy(src, dst, load_sem.at[len(loads)])
        loads[name].start()
    loads["win"].wait()
    loads["wout"].wait()

    win = win_ref[...].astype(F32)
    wout = wout_ref[...].astype(F32)
    for p in range(3):
        own_parts[p] = jnp.concatenate(
            [win[p * 8 : p * 8 + 8], wout[p * 8 : p * 8 + 8]], axis=0
        ).astype(BF16)
    firsts = (first0, first1, first2)
    gathered = (w0, w1, w2)

    def first_copy(p, slot):
        axis = ORDERS[p][0]
        zero, one = SOURCES[axis][slot]
        back = SIZE[axis] - zero - c * (one - zero)
        return pltpu.make_async_remote_copy(
            src_ref=own_parts.at[p], dst_ref=firsts[p].at[slot],
            send_sem=first_ss.at[p, slot], recv_sem=first_rs.at[p, slot],
            device_id=at(**{axis: (me[axis] + back) % SIZE[axis]}), device_id_type=MESH,
        )

    def first_send(p):
        for slot in range(1, len(SOURCES[ORDERS[p][0]])):
            first_copy(p, slot).start()

        @pl.when(c == 1)
        def _():
            first_copy(p, 0).start()

        @pl.when(c == 0)
        def _():
            firsts[p][0] = own_parts[p]

    def first_wait(p):
        n = SIZE[ORDERS[p][0]]
        for slot in range(1, n // 2):
            first_copy(p, slot).wait_recv()

        @pl.when(c == 1)
        def _():
            first_copy(p, 0).wait_recv()

        block = firsts[p][...].astype(F32).reshape(n // 2, 2, 8, D)
        at3, at2 = me[ORDERS[p][2]], me[ORDERS[p][1]]
        for side in range(2):
            gathered[p][at3, at2, side] = block[:, side].reshape(n // 2 * 8, D).astype(BF16)

    def first_done(p):
        for slot in range(1, len(SOURCES[ORDERS[p][0]])):
            first_copy(p, slot).wait_send()

        @pl.when(c == 1)
        def _():
            first_copy(p, 0).wait_send()

    def second_copy(p, k):
        _, axis, last = ORDERS[p]
        block = gathered[p].at[me[last], me[axis]]
        return pltpu.make_async_remote_copy(
            src_ref=block, dst_ref=block,
            send_sem=second_ss.at[p, k], recv_sem=second_rs.at[p, k],
            device_id=at(**{axis: (me[axis] + k) % SIZE[axis]}), device_id_type=MESH,
        )

    def ring_copy(p, step, sub, way):
        _, inner, axis = ORDERS[p]
        n = SIZE[axis]
        shift = (n - (step - 1)) if way == 0 else (step - 1)
        block = gathered[p].at[
            (me[axis] + shift) % n, (me[inner] + SIZE[inner] - sub) % SIZE[inner]
        ]
        if step == n // 2:
            block = block.at[way]
        return pltpu.make_async_remote_copy(
            src_ref=block, dst_ref=block,
            send_sem=ring_ss.at[p, step - 1, sub, way],
            recv_sem=ring_rs.at[p, step - 1, sub, way],
            device_id=at(**{axis: (me[axis] + (1 if way == 0 else n - 1)) % n}),
            device_id_type=MESH,
        )

    def ring_send(p, step, sub):
        if step <= SIZE[ORDERS[p][2]] // 2:
            for way in range(2):
                ring_copy(p, step, sub, way).start()

    todo = list(EVENTS)

    def gather(until):
        count = until - len(EVENTS) + len(todo)
        for event in todo[:count]:
            p = event[0]
            if event[1] == 0:
                first_wait(p)
                for k in (1, 3, 2):
                    second_copy(p, k).start()
                ring_send(p, 1, 0)
            elif event[1] == 1:
                second_copy(p, event[2]).wait_recv()
                ring_send(p, 1, event[2])
            else:
                for way in range(2):
                    ring_copy(p, event[2], event[3], way).wait_recv()
                ring_send(p, event[2] + 1, event[3])
        del todo[:count]

    def gather_sent():
        for p in range(3):
            first_done(p)
            for k in range(1, 4):
                second_copy(p, k).wait_send()
            for step in range(1, SIZE[ORDERS[p][2]] // 2 + 1):
                for sub in range(4):
                    for way in range(2):
                        ring_copy(p, step, sub, way).wait_send()

    partner = (1 - c, f, m)

    def pair_copy(i, src, dst):
        return pltpu.make_async_remote_copy(
            src_ref=src, dst_ref=dst, send_sem=pair_ss.at[i], recv_sem=pair_rs.at[i],
            device_id=partner, device_id_type=MESH,
        )

    loads["cidx"].wait()
    pl.semaphore_wait(barrier, 30)
    for p in range(3):
        first_send(p)
    codes_copy = pair_copy(2, cidx_ref, cidx_recv)
    codes_copy.start()

    for name in ("gs", "sp", "fr"):
        loads[name].wait()
    wqkv = jnp.concatenate([sp[...].reshape(3 * HD, D), jnp.zeros((HD, D), BF16)], axis=0)
    gain_space = gs_ref[...].reshape(1, D)

    @pl.loop(0, 4)
    def _(i):
        rows = pl.ds(pl.multiple_of(i * 256, 256), 256)
        normed = layer_norm(fr[rows, :].astype(F32), gain_space).astype(BF16)
        both = nt_dot(normed, wqkv)
        qk = both[:, :128]
        low = lanes((256, 128)) < HD
        k_s[rows, :] = pltpu.roll(qk, HD, 1).astype(BF16)
        v = both[:, 128:]
        v_s[rows, :] = jnp.where(low, v, 1.0).astype(BF16)
        q = jnp.where(low, qk * (1.0 / math.sqrt(HD)), 0.0).reshape(4, NZ, 8, 128)
        for to_m in range(NZ):
            q_s[to_m, pl.ds(pl.multiple_of(i * 32, 32), 32), :] = (
                q[:, to_m].reshape(32, 128).astype(BF16)
            )

    def heads_copy(shift):
        dest = (m + shift) % NZ
        return pltpu.make_async_remote_copy(
            src_ref=heads_send.at[dest], dst_ref=heads_recv.at[m],
            send_sem=heads_ss.at[shift], recv_sem=heads_rs.at[shift],
            device_id=(c, f, dest), device_id_type=MESH,
        )

    half = lanes((64, 128)) < HD
    for i, shifts in enumerate(((4, 3), (5, 2), (6, 1), (7, 0))):
        queries = jnp.concatenate([q_s[(m + shift) % NZ] for shift in shifts], axis=0)
        scores = nt_dot(queries, k_s[...])
        weights = jnp.exp(scores - jnp.max(scores, axis=-1, keepdims=True)).astype(BF16)
        mixed = jnp.dot(weights, v_s[...], preferred_element_type=F32)
        turned = pltpu.roll(mixed, HD, 1)
        for j, shift in enumerate(shifts):
            top, bottom = slice(j * 128, j * 128 + 64), slice(j * 128 + 64, j * 128 + 128)
            heads_send[(m + shift) % NZ] = (
                jnp.where(half, mixed[top], turned[bottom])
                / jnp.where(half, turned[top], mixed[bottom])
            ).astype(BF16)
        for shift in shifts:
            if shift:
                heads_copy(shift).start()
        gather(GATHER_AT[i])

    heads_recv[m] = heads_send[m]

    def onehot(codes):
        codes = jnp.broadcast_to(codes, (FRAMES, 8, FRAMES)).reshape(128, FRAMES)
        diagonal = lax.broadcasted_iota(jnp.int32, (128, FRAMES), 0) // 8 == lanes((128, FRAMES))
        codes = jnp.sum(jnp.where(diagonal, codes, 0), axis=1, keepdims=True)
        return (codes == lanes((128, CODES))).astype(F32).astype(BF16)

    def count_copy(k):
        dest = (m + k) % NZ
        return pltpu.make_async_remote_copy(
            src_ref=count_send.at[dest], dst_ref=count_recv.at[k], send_sem=count_ss.at[k],
            recv_sem=count_rs.at[k], device_id=(c, f, dest), device_id_type=MESH,
        )

    def all_count_copy(k):
        return pltpu.make_async_remote_copy(
            src_ref=count_all.at[f], dst_ref=count_all.at[f], send_sem=all_count_ss.at[k],
            recv_sem=all_count_rs.at[k], device_id=frame_peer(k), device_id_type=MESH,
        )

    codes_copy.wait_recv()
    hot[:128] = onehot(cidx_recv[...])
    hot[128:] = onehot(cidx_ref[...])
    counts = jnp.dot(jnp.ones((16, 256), BF16), hot[...], preferred_element_type=F32)
    for dest in range(NZ):
        count_send[dest] = counts[:, dest * 128 : dest * 128 + 128].astype(BF16)
    for k in range(1, NZ):
        count_copy(k).start()
    count_recv[0] = count_send[m]
    gather(GATHER_AT[4])
    for k in range(1, NZ):
        heads_copy(k).wait_recv()

    side = lanes((64, 128)) < HD
    upper, lower = [], []
    for i in range(NZ // 2):
        even = heads_recv[2 * i].astype(F32)
        odd = heads_recv[2 * i + 1].astype(F32)
        upper.append(jnp.where(side, even, pltpu.roll(odd, HD, 1)))
        lower.append(jnp.where(side, pltpu.roll(even, HD, 1), odd))
    heads_all = jnp.concatenate(
        [jnp.concatenate(upper, axis=1), jnp.concatenate(lower, axis=1)], axis=0
    ).astype(BF16)
    own = []
    for i in range(FRAMES):
        pair = fr[pl.ds(pl.multiple_of(i * 64 + (m // 2) * 16, 16), 16), :].astype(F32)
        own.append(jnp.where(m % 2 == 0, pair[:8], pair[8:]))
    loads["so"].wait()
    after_space = jnp.concatenate(own, axis=0) + jnp.dot(
        heads_all, so[...], preferred_element_type=F32
    )
    split = after_space.reshape(FRAMES, 8, D)
    rows_send[...] = jnp.concatenate([split[:, :, :HALF], split[:, :, HALF:]], axis=1).astype(BF16)

    def rows_copy(k):
        peer = frame_peer(k)
        return pltpu.make_async_remote_copy(
            src_ref=rows_send.at[peer[1]], dst_ref=rows_recv.at[f],
            send_sem=rows_ss.at[k], recv_sem=rows_rs.at[k],
            device_id=peer, device_id_type=MESH,
        )

    for k in FRAME_ORDER:
        rows_copy(k).start()

    rows_recv[f] = rows_send[f]
    for k in range(1, NZ):
        count_copy(k).wait_recv()
    counts = jnp.sum(count_recv[...].astype(F32), axis=0)
    upper = jnp.floor(counts[:8] * (1.0 / 256.0))
    count_all[f] = jnp.concatenate([counts[8:] - 256.0 * upper, upper], axis=0).astype(BF16)

    for k in FRAME_ORDER:
        all_count_copy(k).start()

    gather(GATHER_AT[5])

    for k in reversed(FRAME_ORDER):
        rows_copy(k).wait_recv()

    for name in ("gt", "tp", "to", "gm", "cproj"):
        loads[name].wait()
    arrived = rows_recv[...].astype(F32)
    after_space = jnp.concatenate([arrived[:, :8], arrived[:, 8:]], axis=2).reshape(128, D)
    time_in = layer_norm(after_space, gt_ref[...].reshape(1, D)).astype(BF16)
    tq = jnp.dot(time_in, tp[0], preferred_element_type=F32) * (1.0 / math.sqrt(HD))
    tk = jnp.dot(time_in, tp[1], preferred_element_type=F32).astype(BF16)
    tv = jnp.dot(time_in, tp[2], preferred_element_type=F32).astype(BF16)
    tq = tq.astype(BF16)
    gather(GATHER_AT[6])
    row = lax.broadcasted_iota(jnp.int32, (128, 128), 0)
    col = lax.broadcasted_iota(jnp.int32, (128, 128), 1)
    seen = ((row % 8 == col % 8) & (col // 8 <= row // 8))[None]
    low = col < HD
    none = jnp.zeros((128, 128), BF16)
    ones = jnp.ones((128, 128), BF16)
    cuts = [slice(i * 128, i * 128 + 128) for i in range(T_HEADS // 2)]
    scores = jnp.concatenate(
        [
            nt_dot(
                jnp.concatenate(
                    [jnp.where(low, tq[:, cut], none), jnp.where(low, none, tq[:, cut])], axis=0
                ),
                tk[:, cut],
            )
            for cut in cuts
        ],
        axis=0,
    ).reshape(T_HEADS, 128, 128)
    scores = jnp.where(seen, scores, -jnp.inf)
    weights = jnp.exp(scores - jnp.max(scores, axis=-1, keepdims=True)).astype(BF16)
    gather(GATHER_AT[7])
    pieces = []
    for i, cut in enumerate(cuts):
        both = jnp.dot(
            weights[2 * i : 2 * i + 2].reshape(256, 128),
            jnp.concatenate([tv[:, cut], ones], axis=1),
            preferred_element_type=F32,
        )
        both = both[:, :128] / both[:, 128:]
        pieces.append(jnp.where(low, both[:128], both[128:]).astype(BF16))
    gather(GATHER_AT[8])
    time_heads = jnp.concatenate(pieces, axis=1)
    after_time = after_space + jnp.dot(time_heads, to[...], preferred_element_type=F32)
    gather(GATHER_AT[9])
    act_send[...] = layer_norm(after_time, gm_ref[...].reshape(1, D)).astype(BF16)

    act_copy = pair_copy(0, act_send, act_recv)
    act_copy.start()
    act_copy.wait_recv()
    act = jnp.concatenate([act_recv[...], act_send[...]], axis=0)
    partial = jnp.zeros((256, D), F32)
    for until, group_of in MLP_GROUPS:
        gather(until)
        w_in, w_out = [], []
        for p, steps in group_of:
            for step in steps:
                block = gathered[p][(me[ORDERS[p][2]] + step) % SIZE[ORDERS[p][2]]]
                w_in.append(block[:, 0].reshape(-1, D))
                w_out.append(block[:, 1].reshape(-1, D))
        hidden = gelu(nt_dot(act, jnp.concatenate(w_in, axis=0))).astype(BF16)
        partial += jnp.dot(hidden, jnp.concatenate(w_out, axis=0), preferred_element_type=F32)

    def red_copy(k):
        peer = group_peer(k)
        return pltpu.make_async_remote_copy(
            src_ref=red_send.at[peer[0] * NZ + peer[2]], dst_ref=red_recv.at[k],
            send_sem=red_ss.at[k], recv_sem=red_rs.at[k], device_id=peer, device_id_type=MESH,
        )

    after_time = after_time + partial[128:]
    share = jnp.concatenate([partial[:128], after_time], axis=0).astype(BF16)
    vecs = nt_dot(cproj_ref[...], share)
    high = vecs.astype(BF16)
    rest = (vecs - high.astype(F32)).astype(BF16)
    sums = jnp.dot(
        jnp.concatenate([high, rest], axis=0), hot[...], preferred_element_type=F32
    )
    sums = sums[:32] + sums[32:]
    for dest in range(16):
        low_row, low_lane = dest // NZ * 16, dest % NZ * 128
        red_send[dest] = sums[low_row : low_row + 16, low_lane : low_lane + 128].astype(BF16)

    for k in GROUP_ORDER:
        red_copy(k).start()

    back_send[...] = partial[:128]
    back_copy = pair_copy(1, back_send, back_recv)
    back_copy.start()

    def tot_copy(k):
        return pltpu.make_async_remote_copy(
            src_ref=tot_all.at[f], dst_ref=tot_all.at[f], send_sem=tot_ss.at[k],
            recv_sem=tot_rs.at[k], device_id=frame_peer(k), device_id_type=MESH,
        )

    def mean_copy(k):
        return pltpu.make_async_remote_copy(
            src_ref=mean_send, dst_ref=mean_recv.at[group], send_sem=fin_ss.at[k],
            recv_sem=fin_rs.at[k], device_id=group_peer(k), device_id_type=MESH,
        )

    gather_sent()
    red_recv[0] = red_send[group]

    for k in reversed(GROUP_ORDER):
        red_copy(k).wait_recv()

    tot_all[f] = jnp.sum(red_recv[...].astype(F32), axis=0).astype(BF16)

    for k in FRAME_ORDER:
        tot_copy(k).start()

    back_copy.wait_recv()
    outputs = (after_time + back_recv[...]).reshape(FRAMES, 8, D)
    out_s[0] = outputs.astype(BF16)
    out_copy = pltpu.make_async_copy(out_s, out_hbm, load_sem.at[0])
    out_copy.start()
    for k in range(1, NZ):
        heads_copy(k).wait_send()
        count_copy(k).wait_send()
    for copy in (codes_copy, act_copy, back_copy):
        copy.wait_send()

    @pl.loop(1, 16)
    def _(k):
        rows_copy(k).wait_send()
        red_copy(k).wait_send()
        all_count_copy(k).wait_send()
        all_count_copy(k).wait_recv()

    counts = jnp.sum(count_all[...].astype(F32), axis=0)
    counts = jnp.maximum(counts[:8] + 256.0 * counts[8:], 1.0)
    counts = jnp.concatenate([counts, counts], axis=0)

    for k in reversed(FRAME_ORDER):
        tot_copy(k).wait_recv()

    means = (jnp.sum(tot_all[...].astype(F32), axis=0) / counts).astype(BF16)
    mean_send[...] = means
    mean_recv[group] = means

    for k in GROUP_ORDER:
        mean_copy(k).start()

    @pl.loop(1, 16)
    def _(k):
        tot_copy(k).wait_send()
        mean_copy(k).wait_send()

    out_copy.wait()

    for k in reversed(GROUP_ORDER):
        mean_copy(k).wait_recv()

    for g in range(16):
        cut = slice(g % NZ * 128, g % NZ * 128 + 128)
        means_ref[g // NZ * 16 : g // NZ * 16 + 16, cut] = mean_recv[g].astype(F32)


def shards(*args):
    args = list(args)
    args[2] = args[2].swapaxes(1, 2)
    args[10] = args[10].T
    args[11] = args[11].swapaxes(1, 2)
    args = [pltpu.with_memory_space_constraint(arg, pltpu.HBM) for arg in args]
    vmem = pl.BlockSpec(memory_space=pltpu.VMEM)
    hbm = pl.BlockSpec(memory_space=pltpu.HBM)
    dma = pltpu.SemaphoreType.DMA
    scratch = [
        pltpu.VMEM((POS, D), BF16),
        pltpu.VMEM((D,), F32),
        pltpu.VMEM((3, HD, D), BF16),
        pltpu.VMEM((512, D), BF16),
        pltpu.VMEM((D,), F32),
        pltpu.VMEM((3, D, D), BF16),
        pltpu.VMEM((D, D), BF16),
        pltpu.VMEM((D,), F32),
        pltpu.VMEM((24, D), BF16),
        pltpu.VMEM((24, D), BF16),
        pltpu.VMEM((32, D), BF16),
        pltpu.VMEM((1, 8, FRAMES), jnp.int32),
        pltpu.VMEM((NZ, 128, 128), BF16),
        pltpu.VMEM((POS, 128), BF16),
        pltpu.VMEM((POS, 128), BF16),
        pltpu.VMEM((NZ, 64, 128), BF16),
        pltpu.VMEM((NZ, 64, 128), BF16),
        pltpu.VMEM((FRAMES, 16, HALF), BF16),
        pltpu.VMEM((FRAMES, 16, HALF), BF16),
        pltpu.VMEM((3, 16, D), BF16),
    ]
    scratch += [pltpu.VMEM((SIZE[order[0]] // 2, 16, D), BF16) for order in ORDERS]
    scratch += [
        pltpu.VMEM((SIZE[order[2]], SIZE[order[1]], 2, units, D), BF16)
        for order, units in zip(ORDERS, UNITS)
    ]
    scratch += [
        pltpu.VMEM((1, 8, FRAMES), jnp.int32),
        pltpu.VMEM((256, CODES), BF16),
        pltpu.VMEM((NZ, 16, 128), BF16),
        pltpu.VMEM((NZ, 16, 128), BF16),
        pltpu.VMEM((FRAMES, 16, 128), BF16),
        pltpu.VMEM((128, D), BF16),
        pltpu.VMEM((128, D), BF16),
        pltpu.VMEM((128, D), F32),
        pltpu.VMEM((128, D), F32),
        pltpu.VMEM((1, FRAMES, 8, D), BF16),
        pltpu.VMEM((16, 16, 128), BF16),
        pltpu.VMEM((16, 16, 128), BF16),
        pltpu.VMEM((FRAMES, 16, 128), BF16),
        pltpu.VMEM((16, 128), BF16),
        pltpu.VMEM((16, 16, 128), BF16),
    ]
    scratch += [
        dma((12,)),
        dma((NZ,)), dma((NZ,)),
        dma((FRAMES,)), dma((FRAMES,)),
        dma((3, NZ)), dma((3, NZ)),
        dma((3, 4)), dma((3, 4)),
        dma((3, 4, 4, 2)), dma((3, 4, 4, 2)),
        dma((3,)), dma((3,)),
        dma((16,)), dma((16,)),
        dma((16,)), dma((16,)),
        dma((16,)), dma((16,)),
        dma((NZ,)), dma((NZ,)),
        dma((16,)), dma((16,)),
    ]
    block_out, means = pl.pallas_call(
        block_kernel,
        out_shape=(
            jax.ShapeDtypeStruct((1, FRAMES, 8, D), BF16),
            jax.ShapeDtypeStruct((32, CODES), F32),
        ),
        in_specs=[hbm] * 12,
        out_specs=(hbm, vmem),
        scratch_shapes=scratch,
        compiler_params=pltpu.CompilerParams(
            collective_id=0, has_side_effects=True, vmem_limit_bytes=52 * 1024 * 1024
        ),
    )(*args)
    return block_out, means.T


def solution(mesh):
    placed = (
        P("dp", "frame", None, None),
        P(),
        P(None, None, "mp"),
        P(),
        P(),
        P(),
        P(),
        P(),
        P(("frame", "mp"), None),
        P(("frame", "mp"), None),
        P(),
        P("dp", None, ("frame", "mp")),
    )
    return jax.shard_map(
        shards,
        mesh=mesh,
        in_specs=placed,
        out_specs=(P("dp", None, ("frame", "mp"), None), P()),
        check_vma=False,
    )
```
